256 devices in a mesh: gx: 32 (over z, y), gz: 8 (over x, core).
Axes of the slice: x: 4, y: 4, z: 8, core: 2. Of those that a mesh axis runs over, the one named last changes fastest.
Arguments:
- velocity: float32 [3, 8, 8192, 2048], P(None, None, 'gx', 'gz'), may hold values from -18 to 18
Outputs:
- derivative: float32 [3, 8, 8192, 2048], P(None, None, 'gx', 'gz')
- energy: float32 [3, 8], replicated
The draws below stay inside these ranges and needn't reach their ends.
All inputs are finite; a program needn't handle non-finite values.
Results may differ from the reference program's by a relative error of at most 0.00017.
Values sent between devices are 32-bit elements; how exact they have to be, the bound alone decides.
A program may use at most 64 MiB of HBM per device.

```python
import math
import jax
import jax.numpy as jnp
from jax import lax

PLANES = 8
NX = 8192
NZ = 2048


def draw_velocity(key, part):
    key = jax.random.fold_in(key, 7)
    streamwise = jnp.arange(NX, dtype=jnp.float32)
    spanwise = jnp.arange(NZ, dtype=jnp.float32)
    spread = jnp.exp(0.5 * math.log(3.0) * (streamwise[:, None] / (NX - 1) + spanwise[None, :] / (NZ - 1)))
    rough = jax.random.truncated_normal(key, -6.0, 6.0, (3, PLANES, NX, NZ), jnp.float32)
    return (rough * spread).astype(jnp.float32)


def setup_inputs(seed: int = 0) -> dict:
    key_of = jax.random.split(jax.random.key(seed), 2)
    return {
        "velocity": draw_velocity(jax.random.fold_in(key_of[1], 71), 0),
    }


ALPHA = 1.0 / 3.0
HALF_A = 7.0 / 9.0
QUARTER_B = 1.0 / 36.0


def derive_slice(field):
    right_side = HALF_A * (jnp.roll(field, -1, 0) - jnp.roll(field, 1, 0)) + QUARTER_B * (jnp.roll(field, -2, 0) - jnp.roll(field, 2, 0))
    points = field.shape[0]
    spectrum = jnp.fft.rfft(right_side, axis=0)
    waves = jnp.arange(points // 2 + 1).astype(field.dtype) * (2.0 * jnp.pi / points)
    symbol = 1.0 + 2.0 * ALPHA * jnp.cos(waves)
    result = jnp.fft.irfft(spectrum / symbol[:, None], n=points, axis=0).astype(field.dtype)
    return result, jnp.mean(result * result)


def reference(velocity):
    flat = velocity.reshape(3 * PLANES, NX, NZ)
    results, means = lax.map(derive_slice, flat)
    return results.reshape(velocity.shape), means.reshape(3, PLANES)
```

```python
import functools
import itertools
import math

import jax
import jax.numpy as jnp
import numpy as np
from jax import lax
from jax.experimental import pallas as pl
from jax.experimental.pallas import tpu as pltpu
from jax.sharding import PartitionSpec as P

ALPHA = 1.0 / 3.0
HALF_A = 7.0 / 9.0
QUARTER_B = 1.0 / 36.0

ROOT = (math.sqrt(1.0 - 4.0 * ALPHA * ALPHA) - 1.0) / (2.0 * ALPHA)
SCALE = 1.0 / math.sqrt(1.0 - 4.0 * ALPHA * ALPHA)
TAIL = SCALE * (HALF_A + QUARTER_B * (ROOT + 1.0 / ROOT))
CENTRE = SCALE * (HALF_A + 2.0 * QUARTER_B * ROOT)
BUMP = CENTRE - TAIL
REACH = 96

SIZES = {"x": 4, "y": 4, "z": 8, "core": 2}
PHASES = (("x", "y"), ("z", "core"))
MESH = pl.DeviceIdType.MESH
LANES = 128


def hops(offset, axis):
    return 0 if axis == "core" else min(offset, SIZES[axis] - offset)


def partners(axes):
    gx, gz = lax.axis_index("gx"), lax.axis_index("gz")
    here = {"x": gz // 2, "core": gz % 2, "z": gx // 4, "y": gx % 4}
    offsets = [o for o in itertools.product(*(range(SIZES[a]) for a in axes)) if any(o)]
    offsets.sort(key=lambda o: -sum(hops(v, a) for v, a in zip(o, axes)))
    found = []
    for offset in offsets:
        there = dict(here)
        for axis, value in zip(axes, offset):
            if value:
                there[axis] = (here[axis] + value) % SIZES[axis]
        found.append((there["z"] * 4 + there["y"], there["x"] * 2 + there["core"]))
    return found


def tables(points):
    index = np.arange(points)
    distance = np.abs(index[:, None] - index[None, :])
    matrix = np.where(distance == 0, CENTRE, TAIL * ROOT ** distance.astype(np.float64))
    matrix[:, 0] = 0.0
    matrix[:, points - 1] = 0.0
    reach = np.arange(REACH)
    powers = ROOT ** reach.astype(np.float64)
    head = ROOT ** (reach + 1.0)
    head[0] = head[REACH - 1] = 0.0
    columns = np.stack([powers, powers[::-1], head, head[::-1]])
    columns = np.broadcast_to(columns[:, :, None], (4, REACH, LANES))
    return matrix.astype(np.float32), columns.astype(np.float32)


def column_sum(weights, block):
    w = jnp.concatenate([weights, weights], axis=1)
    return jnp.sum(w * block, axis=0, keepdims=True)


def kernel(
    planes, points, v_hbm, matrix_hbm, column_hbm, d_ref, e_ref,
    v, matrix, high, low, columns, out, got, rows, tots, shares, load_sem, const_sem, halo_send, halo_recv, sum_send, sum_recv,
):
    gx, gz = lax.axis_index("gx"), lax.axis_index("gz")
    ring = lax.axis_size("gx")
    right, left = ((gx + 1) % ring, gz), ((gx + ring - 1) % ring, gz)
    groups = [partners(axes) for axes in PHASES]

    barrier = pltpu.get_barrier_semaphore()
    known = [left, right] + groups[0] + groups[1]
    for device in known:
        pl.semaphore_signal(barrier, inc=1, device_id=device, device_id_type=MESH)

    constants = [
        pltpu.make_async_copy(source, target, const_sem.at[i])
        for i, (source, target) in enumerate(((column_hbm, columns), (matrix_hbm, matrix)))
    ]

    def load(p):
        return pltpu.make_async_copy(v_hbm.at[p], v.at[p], load_sem.at[p])

    constants[0].start()
    for p in range(planes):
        load(p).start()
    constants[1].start()
    constants[0].wait()

    def summarise(p, carry):
        load(p).wait()
        head, tail = v[p, :REACH, :], v[p, points - REACH :, :]
        first, second = head[0:1], head[1:2]
        last, before = tail[REACH - 1 :], tail[REACH - 2 : REACH - 1]
        head = pltpu.roll(head, REACH - 1, 0) - pltpu.roll(head, 1, 0)
        tail = pltpu.roll(tail, REACH - 1, 0) - pltpu.roll(tail, 1, 0)
        one = pl.ds(p, 1)
        out[0, 0, one, :] = first
        out[0, 1, one, :] = column_sum(columns[2], head) + ROOT * (second - first)
        out[1, 0, one, :] = last
        out[1, 1, one, :] = column_sum(columns[3], tail) + ROOT * (last - before)
        rows[0, one, :] = second
        rows[1, one, :] = before
        return carry

    lax.fori_loop(0, planes, summarise, 0)

    pl.semaphore_wait(barrier, len(known))
    halo = [
        pltpu.make_async_remote_copy(
            src_ref=out.at[i], dst_ref=got.at[1 - i], send_sem=halo_send.at[i], recv_sem=halo_recv.at[1 - i],
            device_id=device, device_id_type=MESH,
        )
        for i, device in enumerate((left, right))
    ]
    for copy in halo:
        copy.start()
    constants[1].wait()
    high[...] = matrix[...].astype(jnp.bfloat16)
    low[...] = (matrix[...] - high[...].astype(jnp.float32)).astype(jnp.bfloat16)

    def solve(p, carry):
        block = v[p]
        delta = pltpu.roll(block, points - 1, 0) - pltpu.roll(block, 1, 0)
        coarse = delta.astype(jnp.bfloat16)
        fine = (delta - coarse.astype(jnp.float32)).astype(jnp.bfloat16)
        local = (
            jnp.dot(low[...], coarse, preferred_element_type=jnp.float32)
            + jnp.dot(high[...], fine, preferred_element_type=jnp.float32)
        ) + jnp.dot(high[...], coarse, preferred_element_type=jnp.float32)
        d_ref[p] = local
        one = pl.ds(p, 1)
        rows[2, one, :] = local[0:1]
        rows[3, one, :] = local[points - 1 :]
        rows[4, one, :] = column_sum(columns[0], local[:REACH])
        rows[5, one, :] = column_sum(columns[1], local[points - REACH :])
        rows[6, one, :] = jnp.sum(local * local, axis=0, keepdims=True)
        return carry

    lax.fori_loop(0, planes, solve, 0)

    for copy in halo:
        copy.wait()

    energy = rows[6]
    squares = 1.0 / (1.0 - ROOT * ROOT)
    for side, sign in ((0, 1.0), (1, -1.0)):
        own, inner, edge = out[side, 0], rows[side], got[side, 0]
        jump = sign * (inner - edge)
        total = jump + got[side, 1] + (sign * ROOT) * (own - edge)
        energy = energy + 2.0 * (TAIL * total * rows[4 + side] + BUMP * jump * rows[2 + side])
        energy = energy + (TAIL * TAIL * squares) * total * total
        energy = energy + (2.0 * TAIL * BUMP) * total * jump + (BUMP * BUMP) * jump * jump
        tots[side] = TAIL * total
        tots[2 + side] = BUMP * jump

    energy = jnp.sum(energy[:, :LANES] + energy[:, LANES:], axis=1, keepdims=True)
    chosen = lax.broadcasted_iota(jnp.int32, (planes, LANES), 0) == lax.broadcasted_iota(jnp.int32, (planes, LANES), 1)
    share = jnp.sum(jnp.where(chosen, jnp.broadcast_to(energy, (planes, LANES)), 0.0), axis=0, keepdims=True)

    def send_sums(phase, group):
        n = len(group)
        for i, device in enumerate(group):
            pltpu.make_async_remote_copy(
                src_ref=shares.at[phase, pl.ds(n, 1)], dst_ref=shares.at[phase, pl.ds(i, 1)],
                send_sem=sum_send.at[phase], recv_sem=sum_recv.at[phase],
                device_id=device, device_id_type=MESH,
            ).start()

    def all_of(phase, group, semaphore):
        part = shares.at[phase, pl.ds(0, len(group))]
        return pltpu.make_async_copy(part, part, semaphore.at[phase])

    shares[0, len(groups[0]) : len(groups[0]) + 1, :] = share
    send_sums(0, groups[0])

    def correct(p, carry):
        one = pl.ds(p, 1)
        for side in range(2):
            wide = jnp.concatenate([columns[side], columns[side]], axis=1)
            place = pl.ds(0, REACH) if side == 0 else pl.ds(points - REACH, REACH)
            d_ref[p, place, :] = d_ref[p, place, :] + wide * tots[side, one, :]
        top, bottom = pl.ds(0, 1), pl.ds(points - 1, 1)
        d_ref[p, top, :] = d_ref[p, top, :] + tots[2, one, :]
        d_ref[p, bottom, :] = d_ref[p, bottom, :] + tots[3, one, :]
        return carry

    lax.fori_loop(0, planes, correct, 0)

    all_of(0, groups[0], sum_recv).wait()
    share = jnp.sum(shares[0], axis=0, keepdims=True)
    shares[1, len(groups[1]) : len(groups[1]) + 1, :] = share
    send_sums(1, groups[1])
    all_of(1, groups[1], sum_recv).wait()
    total = jnp.sum(shares[1], axis=0, keepdims=True)
    count = float(points * ring * 2 * LANES * lax.axis_size("gz"))
    e_ref[...] = total * (1.0 / count)
    all_of(0, groups[0], sum_send).wait()
    all_of(1, groups[1], sum_send).wait()


def shards(velocity):
    components, heights, points, spanwise = velocity.shape
    planes = components * heights
    matrix, columns = tables(points)
    whole = pl.BlockSpec(memory_space=pltpu.HBM)
    derivative, energy = pl.pallas_call(
        functools.partial(kernel, planes, points),
        out_shape=(
            pltpu.VMEM((planes, points, spanwise), jnp.float32),
            jax.ShapeDtypeStruct((1, LANES), jnp.float32),
        ),
        in_specs=[whole] * 3,
        out_specs=(pl.BlockSpec(memory_space=pltpu.VMEM), pl.BlockSpec(memory_space=pltpu.VMEM)),
        scratch_shapes=[
            pltpu.VMEM((planes, points, spanwise), jnp.float32),
            pltpu.VMEM((points, points), jnp.float32),
            pltpu.VMEM((points, points), jnp.bfloat16),
            pltpu.VMEM((points, points), jnp.bfloat16),
            pltpu.VMEM((4, REACH, LANES), jnp.float32),
            pltpu.VMEM((2, 2, planes, spanwise), jnp.float32),
            pltpu.VMEM((2, 2, planes, spanwise), jnp.float32),
            pltpu.VMEM((7, planes, spanwise), jnp.float32),
            pltpu.VMEM((4, planes, spanwise), jnp.float32),
            pltpu.VMEM((2, 16, LANES), jnp.float32),
            pltpu.SemaphoreType.DMA((planes,)),
            pltpu.SemaphoreType.DMA((2,)),
            pltpu.SemaphoreType.DMA((2,)),
            pltpu.SemaphoreType.DMA((2,)),
            pltpu.SemaphoreType.DMA((2,)),
            pltpu.SemaphoreType.DMA((2,)),
        ],
        compiler_params=pltpu.CompilerParams(
            collective_id=0, has_side_effects=True, vmem_limit_bytes=24 * 1024 * 1024
        ),
        name="derive",
    )(*(
        pltpu.with_memory_space_constraint(operand, pltpu.HBM)
        for operand in (velocity.reshape(planes, points, spanwise), jnp.asarray(matrix), jnp.asarray(columns))
    ))
    return (
        derivative.reshape(velocity.shape),
        energy[0, :planes].reshape(components, heights),
    )


def solution(mesh):
    return jax.shard_map(
        shards,
        mesh=mesh,
        in_specs=(P(None, None, "gx", "gz"),),
        out_specs=(P(None, None, "gx", "gz"), P()),
        check_vma=False,
    )
```

```python
import functools
import itertools
import math

import jax
import jax.numpy as jnp
import numpy as np
from jax import lax
from jax.experimental import pallas as pl
from jax.experimental.pallas import tpu as pltpu
from jax.sharding import PartitionSpec as P

ALPHA = 1.0 / 3.0
HALF_A = 7.0 / 9.0
QUARTER_B = 1.0 / 36.0

ROOT = (math.sqrt(1.0 - 4.0 * ALPHA * ALPHA) - 1.0) / (2.0 * ALPHA)
SCALE = 1.0 / math.sqrt(1.0 - 4.0 * ALPHA * ALPHA)
TAIL = SCALE * (HALF_A + QUARTER_B * (ROOT + 1.0 / ROOT))
CENTRE = SCALE * (HALF_A + 2.0 * QUARTER_B * ROOT)
BUMP = CENTRE - TAIL
REACH = 96

SIZES = {"x": 4, "y": 4, "z": 8, "core": 2}
PHASES = (("x", "y"), ("z", "core"))
MESH = pl.DeviceIdType.MESH
LANES = 128
PIECE = 4
GROUP = 8


def hops(offset, axis):
    return 0 if axis == "core" else min(offset, SIZES[axis] - offset)


def partners(axes):
    gx, gz = lax.axis_index("gx"), lax.axis_index("gz")
    here = {"x": gz // 2, "core": gz % 2, "z": gx // 4, "y": gx % 4}
    offsets = [o for o in itertools.product(*(range(SIZES[a]) for a in axes)) if any(o)]
    offsets.sort(key=lambda o: -sum(hops(v, a) for v, a in zip(o, axes)))
    found = []
    for offset in offsets:
        there = dict(here)
        for axis, value in zip(axes, offset):
            if value:
                there[axis] = (here[axis] + value) % SIZES[axis]
        found.append((there["z"] * 4 + there["y"], there["x"] * 2 + there["core"]))
    return found


def tables(points):
    index = np.arange(points)
    distance = np.abs(index[:, None] - index[None, :])
    matrix = np.where(distance == 0, CENTRE, TAIL * ROOT ** distance.astype(np.float64))
    matrix[:, 0] = 0.0
    matrix[:, points - 1] = 0.0
    reach = np.arange(REACH)
    powers = ROOT ** reach.astype(np.float64)
    head = ROOT ** (reach + 1.0)
    head[0] = head[REACH - 1] = 0.0
    columns = np.stack([powers, powers[::-1], head, head[::-1]])
    columns = np.broadcast_to(columns[:, :, None], (4, REACH, LANES))
    return matrix.astype(np.float32), columns.astype(np.float32)


def column_sum(weights, block):
    w = jnp.concatenate([weights, weights], axis=1)
    return jnp.sum(w * block, axis=0, keepdims=True)


def kernel(
    planes, points, v_hbm, matrix_hbm, column_hbm, d_ref, e_ref,
    v, matrix, split, columns, out, got, rows, tots, shares, load_sem, const_sem, halo_send, halo_recv, sum_send, sum_recv,
):
    gx, gz = lax.axis_index("gx"), lax.axis_index("gz")
    ring = lax.axis_size("gx")
    right, left = ((gx + 1) % ring, gz), ((gx + ring - 1) % ring, gz)
    groups = [partners(axes) for axes in PHASES]

    barrier = pltpu.get_barrier_semaphore()
    known = [left, right] + groups[0] + groups[1]
    for device in known:
        pl.semaphore_signal(barrier, inc=1, device_id=device, device_id_type=MESH)

    constants = [
        pltpu.make_async_copy(source, target, const_sem.at[i])
        for i, (source, target) in enumerate(((column_hbm, columns), (matrix_hbm, matrix)))
    ]

    def load(i):
        part = pl.ds(i * PIECE, PIECE)
        return pltpu.make_async_copy(v_hbm.at[part], v.at[part], load_sem.at[i])

    constants[0].start()
    for i in range(planes // PIECE):
        load(i).start()
    constants[1].start()
    constants[0].wait()

    def summarise(p):
        head, tail = v[p, :REACH, :], v[p, points - REACH :, :]
        first, second = head[0:1], head[1:2]
        last, before = tail[REACH - 1 :], tail[REACH - 2 : REACH - 1]
        head = pltpu.roll(head, REACH - 1, 0) - pltpu.roll(head, 1, 0)
        tail = pltpu.roll(tail, REACH - 1, 0) - pltpu.roll(tail, 1, 0)
        one = pl.ds(p, 1)
        out[0, 0, one, :] = first
        out[0, 1, one, :] = column_sum(columns[2], head) + ROOT * (second - first)
        out[1, 0, one, :] = last
        out[1, 1, one, :] = column_sum(columns[3], tail) + ROOT * (last - before)
        rows[0, one, :] = second
        rows[1, one, :] = before

    def summarise_piece(i, carry):
        load(i).wait()
        for k in range(PIECE):
            summarise(i * PIECE + k)
        return carry

    lax.fori_loop(0, planes // PIECE, summarise_piece, 0)

    pl.semaphore_wait(barrier, len(known))
    halo = [
        pltpu.make_async_remote_copy(
            src_ref=out.at[i], dst_ref=got.at[1 - i], send_sem=halo_send.at[i], recv_sem=halo_recv.at[1 - i],
            device_id=device, device_id_type=MESH,
        )
        for i, device in enumerate((left, right))
    ]
    for copy in halo:
        copy.start()
    constants[1].wait()
    high = matrix[...].astype(jnp.bfloat16)
    split[:, :points] = (matrix[...] - high.astype(jnp.float32)).astype(jnp.bfloat16)
    split[:, points : 2 * points] = high
    split[:, 2 * points :] = high

    def solve(p):
        block = v[p]
        delta = pltpu.roll(block, points - 1, 0) - pltpu.roll(block, 1, 0)
        coarse = delta.astype(jnp.bfloat16)
        fine = (delta - coarse.astype(jnp.float32)).astype(jnp.bfloat16)
        local = jnp.dot(
            split[...], jnp.concatenate([coarse, fine, coarse], axis=0), preferred_element_type=jnp.float32
        )
        d_ref[p] = local
        one = pl.ds(p, 1)
        rows[2, one, :] = local[0:1]
        rows[3, one, :] = local[points - 1 :]
        rows[4, one, :] = column_sum(columns[0], local[:REACH])
        rows[5, one, :] = column_sum(columns[1], local[points - REACH :])
        rows[6, one, :] = jnp.sum(local * local, axis=0, keepdims=True)

    def solve_group(i, carry):
        for k in range(GROUP):
            solve(i * GROUP + k)
        return carry

    lax.fori_loop(0, planes // GROUP, solve_group, 0)

    for copy in halo:
        copy.wait()

    energy = rows[6]
    squares = 1.0 / (1.0 - ROOT * ROOT)
    for side, sign in ((0, 1.0), (1, -1.0)):
        own, inner, edge = out[side, 0], rows[side], got[side, 0]
        jump = sign * (inner - edge)
        total = jump + got[side, 1] + (sign * ROOT) * (own - edge)
        energy = energy + 2.0 * (TAIL * total * rows[4 + side] + BUMP * jump * rows[2 + side])
        energy = energy + (TAIL * TAIL * squares) * total * total
        energy = energy + (2.0 * TAIL * BUMP) * total * jump + (BUMP * BUMP) * jump * jump
        tots[side] = TAIL * total
        tots[2 + side] = BUMP * jump

    energy = jnp.sum(energy[:, :LANES] + energy[:, LANES:], axis=1, keepdims=True)
    chosen = lax.broadcasted_iota(jnp.int32, (planes, LANES), 0) == lax.broadcasted_iota(jnp.int32, (planes, LANES), 1)
    share = jnp.sum(jnp.where(chosen, jnp.broadcast_to(energy, (planes, LANES)), 0.0), axis=0, keepdims=True)

    def send_sums(phase, group):
        n = len(group)
        for i, device in enumerate(group):
            pltpu.make_async_remote_copy(
                src_ref=shares.at[phase, pl.ds(n, 1)], dst_ref=shares.at[phase, pl.ds(i, 1)],
                send_sem=sum_send.at[phase], recv_sem=sum_recv.at[phase],
                device_id=device, device_id_type=MESH,
            ).start()

    def all_of(phase, group, semaphore):
        part = shares.at[phase, pl.ds(0, len(group))]
        return pltpu.make_async_copy(part, part, semaphore.at[phase])

    shares[0, len(groups[0]) : len(groups[0]) + 1, :] = share
    send_sums(0, groups[0])

    def correct(p, carry):
        one = pl.ds(p, 1)
        for side in range(2):
            wide = jnp.concatenate([columns[side], columns[side]], axis=1)
            place = pl.ds(0, REACH) if side == 0 else pl.ds(points - REACH, REACH)
            d_ref[p, place, :] = d_ref[p, place, :] + wide * tots[side, one, :]
        top, bottom = pl.ds(0, 1), pl.ds(points - 1, 1)
        d_ref[p, top, :] = d_ref[p, top, :] + tots[2, one, :]
        d_ref[p, bottom, :] = d_ref[p, bottom, :] + tots[3, one, :]
        return carry

    lax.fori_loop(0, planes, correct, 0)

    all_of(0, groups[0], sum_recv).wait()
    share = jnp.sum(shares[0], axis=0, keepdims=True)
    shares[1, len(groups[1]) : len(groups[1]) + 1, :] = share
    send_sums(1, groups[1])
    all_of(1, groups[1], sum_recv).wait()
    total = jnp.sum(shares[1], axis=0, keepdims=True)
    count = float(points * ring * 2 * LANES * lax.axis_size("gz"))
    total = total * (1.0 / count)
    per_row = e_ref.shape[1]
    for i in range(e_ref.shape[0]):
        e_ref[i : i + 1, :] = total[:, i * per_row : (i + 1) * per_row]
    all_of(0, groups[0], sum_send).wait()
    all_of(1, groups[1], sum_send).wait()


def deliver(d_vmem, e_vmem, d_hbm, e_ref, sem):
    copy = pltpu.make_async_copy(d_vmem, d_hbm, sem)
    copy.start()
    e_ref[...] = e_vmem[...]
    copy.wait()


def shards(velocity):
    components, heights, points, spanwise = velocity.shape
    planes = components * heights
    matrix, columns = tables(points)
    whole = pl.BlockSpec(memory_space=pltpu.HBM)
    derivative, energy = pl.pallas_call(
        functools.partial(kernel, planes, points),
        out_shape=(
            pltpu.VMEM((planes, points, spanwise), jnp.float32),
            pltpu.VMEM((components, heights), jnp.float32),
        ),
        in_specs=[whole] * 3,
        out_specs=(pl.BlockSpec(memory_space=pltpu.VMEM), pl.BlockSpec(memory_space=pltpu.VMEM)),
        scratch_shapes=[
            pltpu.VMEM((planes, points, spanwise), jnp.float32),
            pltpu.VMEM((points, points), jnp.float32),
            pltpu.VMEM((points, 3 * points), jnp.bfloat16),
            pltpu.VMEM((4, REACH, LANES), jnp.float32),
            pltpu.VMEM((2, 2, planes, spanwise), jnp.float32),
            pltpu.VMEM((2, 2, planes, spanwise), jnp.float32),
            pltpu.VMEM((7, planes, spanwise), jnp.float32),
            pltpu.VMEM((4, planes, spanwise), jnp.float32),
            pltpu.VMEM((2, 16, LANES), jnp.float32),
            pltpu.SemaphoreType.DMA((planes // PIECE,)),
            pltpu.SemaphoreType.DMA((2,)),
            pltpu.SemaphoreType.DMA((2,)),
            pltpu.SemaphoreType.DMA((2,)),
            pltpu.SemaphoreType.DMA((2,)),
            pltpu.SemaphoreType.DMA((2,)),
        ],
        compiler_params=pltpu.CompilerParams(
            collective_id=0, has_side_effects=True, vmem_limit_bytes=24 * 1024 * 1024
        ),
        name="derive",
    )(*(
        pltpu.with_memory_space_constraint(operand, pltpu.HBM)
        for operand in (velocity.reshape(planes, points, spanwise), jnp.asarray(matrix), jnp.asarray(columns))
    ))
    derivative, energy = pl.pallas_call(
        deliver,
        out_shape=(
            jax.ShapeDtypeStruct(derivative.shape, jnp.float32),
            jax.ShapeDtypeStruct(energy.shape, jnp.float32),
        ),
        in_specs=[pl.BlockSpec(memory_space=pltpu.VMEM)] * 2,
        out_specs=(whole, pl.BlockSpec(memory_space=pltpu.VMEM)),
        scratch_shapes=[pltpu.SemaphoreType.DMA],
        compiler_params=pltpu.CompilerParams(vmem_limit_bytes=4 * 1024 * 1024),
        name="deliver",
    )(derivative, energy)
    return derivative.reshape(velocity.shape), energy


def solution(mesh):
    return jax.shard_map(
        shards,
        mesh=mesh,
        in_specs=(P(None, None, "gx", "gz"),),
        out_specs=(P(None, None, "gx", "gz"), P()),
        check_vma=False,
    )
```

```python
import functools
import itertools
import math

import jax
import jax.numpy as jnp
import numpy as np
from jax import lax
from jax.experimental import pallas as pl
from jax.experimental.pallas import tpu as pltpu
from jax.sharding import PartitionSpec as P

ALPHA = 1.0 / 3.0
HALF_A = 7.0 / 9.0
QUARTER_B = 1.0 / 36.0

ROOT = (math.sqrt(1.0 - 4.0 * ALPHA * ALPHA) - 1.0) / (2.0 * ALPHA)
SCALE = 1.0 / math.sqrt(1.0 - 4.0 * ALPHA * ALPHA)
TAIL = SCALE * (HALF_A + QUARTER_B * (ROOT + 1.0 / ROOT))
CENTRE = SCALE * (HALF_A + 2.0 * QUARTER_B * ROOT)
BUMP = CENTRE - TAIL
REACH = 96

SIZES = {"x": 4, "y": 4, "z": 8, "core": 2}
PHASES = (("x", "y"), ("z", "core"))
AHEAD = {"x": 0, "y": 0, "z": 0, "core": 1}
FAR = range(3, 8)
MESH = pl.DeviceIdType.MESH
LANES = 128
ROW = SIZES["x"] * SIZES["core"]
PIECE = 4
GROUP = 8
MIB = 1024 * 1024


def around():
    gx, gz = lax.axis_index("gx"), lax.axis_index("gz")
    here = {"z": lax.div(gx, 4), "y": lax.rem(gx, 4), "x": lax.div(gz, 2), "core": lax.rem(gz, 2)}

    @functools.cache
    def moved(axis, offset):
        return lax.rem(here[axis] + offset, SIZES[axis]) if offset else here[axis]

    @functools.cache
    def paired(major, minor, one, two):
        if not (one or two):
            return gx if major == "z" else gz
        return moved(major, one) * SIZES[minor] + moved(minor, two)

    def at(x=0, y=0, z=0, core=0):
        return (
            paired("z", "y", z % SIZES["z"], y % SIZES["y"]),
            paired("x", "core", x % SIZES["x"], core % SIZES["core"]),
        )

    return at


def hops(offset, axis):
    return 0 if axis == "core" else min(offset, SIZES[axis] - offset)


def partners(at, axes):
    offsets = [o for o in itertools.product(*(range(SIZES[a]) for a in axes)) if any(o)]
    offsets.sort(key=lambda o: -sum(hops(v, a) for v, a in zip(o, axes)))
    return [at(**dict(zip(axes, offset))) for offset in offsets]


def far_devices():
    found = []
    for z, y, x, core in itertools.product(FAR, *(range(SIZES[a]) for a in ("y", "x", "core"))):
        place = {"x": x, "y": y, "z": z, "core": core}
        away = sum(hops(abs(place[a] - AHEAD[a]), a) for a in place)
        found.append((-away, z * SIZES["y"] + y, x * SIZES["core"] + core))
    return [there for _, *there in sorted(found)]


def tables(points):
    index = np.arange(points)
    distance = np.abs(index[:, None] - index[None, :])
    matrix = np.where(distance == 0, CENTRE, TAIL * ROOT ** distance.astype(np.float64))
    matrix[:, 0] = 0.0
    matrix[:, points - 1] = 0.0
    reach = np.arange(REACH)
    powers = ROOT ** reach.astype(np.float64)
    head = ROOT ** (reach + 1.0)
    head[0] = head[REACH - 1] = 0.0
    columns = np.stack([powers, powers[::-1], head, head[::-1]])
    columns = np.broadcast_to(columns[:, :, None], (4, REACH, LANES))
    return matrix.astype(np.float32), columns.astype(np.float32)


def column_sum(weights, block):
    w = jnp.concatenate([weights, weights], axis=1)
    return jnp.sum(w * block, axis=0, keepdims=True)


def derive(
    v_hbm, matrix_hbm, column_hbm, d_ref, e_ref,
    v, matrix, split, columns, out, got, rows, tots, shares, load_sem, const_sem, halo_send, halo_recv, sum_send, sum_recv,
    direct, extra, direct_send, direct_recv,
):
    planes, points, _ = v.shape
    parts, per_part = out.shape[1], out.shape[3]
    gx, gz = lax.axis_index("gx"), lax.axis_index("gz")
    ring = lax.axis_size("gx")
    sides = ((lax.rem(gx + ring - 1, ring), gz), (lax.rem(gx + 1, ring), gz))

    at = around()
    groups = [partners(at, axes) for axes in PHASES]

    shares[1] = jnp.zeros_like(shares[1])
    extra[...] = jnp.zeros_like(extra)

    constants = [
        pltpu.make_async_copy(source, target, const_sem.at[i])
        for i, (source, target) in enumerate(((column_hbm, columns), (matrix_hbm, matrix)))
    ]

    def load(i):
        piece = pl.ds(i * PIECE, PIECE)
        return pltpu.make_async_copy(v_hbm.at[piece], v.at[piece], load_sem.at[i])

    constants[0].start()
    for i in range(planes // PIECE):
        load(i).start()
    constants[1].start()

    def signal(semaphore, there):
        pl.semaphore_signal(semaphore, inc=1, device_id=there, device_id_type=MESH)

    barrier = pltpu.get_barrier_semaphore()
    known = groups[1] + groups[0] + list(sides)
    for there in known:
        signal(barrier, there)

    first = (AHEAD["z"] * SIZES["y"] + AHEAD["y"], AHEAD["x"] * SIZES["core"] + AHEAD["core"])
    is_first = (gx == first[0]) & (gz == first[1])
    low, high_end = FAR.start * SIZES["y"], FAR.stop * SIZES["y"]
    is_far = (gx >= low) & (gx < high_end)

    @pl.when(is_first)
    def _():
        for there in far_devices():
            signal(barrier, there)

    constants[0].wait()

    def summarise(part, k):
        p = part * per_part + k
        head, tail = v[p, :REACH, :], v[p, points - REACH :, :]
        first, second = head[0:1], head[1:2]
        last, before = tail[REACH - 1 :], tail[REACH - 2 : REACH - 1]
        head = pltpu.roll(head, REACH - 1, 0) - pltpu.roll(head, 1, 0)
        tail = pltpu.roll(tail, REACH - 1, 0) - pltpu.roll(tail, 1, 0)
        one, row = pl.ds(p, 1), pl.ds(k, 1)
        out[0, part, 0, row, :] = first
        out[0, part, 1, row, :] = column_sum(columns[2], head) + ROOT * (second - first)
        out[1, part, 0, row, :] = last
        out[1, part, 1, row, :] = column_sum(columns[3], tail) + ROOT * (last - before)
        rows[0, one, :] = second
        rows[1, one, :] = before

    def halo(part, i):
        return pltpu.make_async_remote_copy(
            src_ref=out.at[i, part], dst_ref=got.at[1 - i, part],
            send_sem=halo_send.at[i, part], recv_sem=halo_recv.at[1 - i, part],
            device_id=sides[i], device_id_type=MESH,
        )

    for part in range(parts):

        def summarise_piece(i, carry):
            load(part * (per_part // PIECE) + i).wait()
            for k in range(PIECE):
                summarise(part, i * PIECE + k)
            return carry

        lax.fori_loop(0, per_part // PIECE, summarise_piece, 0)

    pl.semaphore_wait(barrier, len(known) + is_far.astype(jnp.int32))
    for part in range(parts):
        for i in range(2):
            halo(part, i).start()
    constants[1].wait()
    high = matrix[...].astype(jnp.bfloat16)
    split[:, :points] = (matrix[...] - high.astype(jnp.float32)).astype(jnp.bfloat16)
    split[:, points : 2 * points] = high
    split[:, 2 * points :] = high
    def solve(p):
        block = v[p]
        delta = pltpu.roll(block, points - 1, 0) - pltpu.roll(block, 1, 0)
        coarse = delta.astype(jnp.bfloat16)
        fine = (delta - coarse.astype(jnp.float32)).astype(jnp.bfloat16)
        local = jnp.dot(
            split[...], jnp.concatenate([coarse, fine, coarse], axis=0), preferred_element_type=jnp.float32
        )
        d_ref[p] = local
        one = pl.ds(p, 1)
        rows[2, one, :] = local[0:1]
        rows[3, one, :] = local[points - 1 :]
        rows[4, one, :] = column_sum(columns[0], local[:REACH])
        rows[5, one, :] = column_sum(columns[1], local[points - REACH :])
        rows[6, one, :] = jnp.sum(local * local, axis=0, keepdims=True)

    def solve_group(i, carry):
        for k in range(GROUP):
            solve(i * GROUP + k)
        return carry

    lax.fori_loop(0, planes // GROUP, solve_group, 0)

    squares = 1.0 / (1.0 - ROOT * ROOT)
    sums = []
    for part in range(parts):
        span = pl.ds(part * per_part, per_part)
        energy = rows[6, span, :]
        for i in range(2):
            halo(part, i).wait()
        for side, sign in ((0, 1.0), (1, -1.0)):
            own, inner, edge = out[side, part, 0], rows[side, span, :], got[side, part, 0]
            jump = sign * (inner - edge)
            total = jump + got[side, part, 1] + (sign * ROOT) * (own - edge)
            energy = energy + 2.0 * (TAIL * total * rows[4 + side, span, :] + BUMP * jump * rows[2 + side, span, :])
            energy = energy + (TAIL * TAIL * squares) * total * total
            energy = energy + (2.0 * TAIL * BUMP) * total * jump + (BUMP * BUMP) * jump * jump
            tots[side, span, :] = TAIL * total
            tots[2 + side, span, :] = BUMP * jump
        sums.append(jnp.sum(energy[:, :LANES] + energy[:, LANES:], axis=1, keepdims=True))

    chosen = lax.broadcasted_iota(jnp.int32, (planes, LANES), 0) == lax.broadcasted_iota(jnp.int32, (planes, LANES), 1)
    energy = jnp.broadcast_to(jnp.concatenate(sums, axis=0), (planes, LANES))
    share = jnp.sum(jnp.where(chosen, energy, 0.0), axis=0, keepdims=True)

    n_far = direct.shape[0]

    def send_direct():
        return pltpu.make_async_remote_copy(
            src_ref=shares.at[0, pl.ds(len(groups[0]), 1)], dst_ref=direct.at[pl.ds((gx - low) * ROW + gz, 1)],
            send_sem=direct_send, recv_sem=direct_recv, device_id=first, device_id_type=MESH,
        )

    def send_sum(phase, i):
        group = groups[phase]
        return pltpu.make_async_remote_copy(
            src_ref=shares.at[phase, pl.ds(len(group), 1)], dst_ref=shares.at[phase, pl.ds(i, 1)],
            send_sem=sum_send.at[phase], recv_sem=sum_recv.at[phase],
            device_id=group[i], device_id_type=MESH,
        )

    def rows_of(phase, count, semaphore):
        part = shares.at[phase, pl.ds(0, count)]
        return pltpu.make_async_copy(part, part, semaphore.at[phase])

    n_near, n_level = len(groups[0]), len(groups[1])
    skips = is_far & (lax.rem(gx, SIZES["y"]) == AHEAD["y"]) & (lax.div(gz, SIZES["core"]) == AHEAD["x"])
    n_skip = len(FAR) * SIZES["core"]

    shares[0, n_near : n_near + 1, :] = share

    @pl.when(is_far)
    def _():
        send_direct().start()

    for i in range(n_near):
        send_sum(0, i).start()

    def correct(p, carry):
        one = pl.ds(p, 1)
        for side in range(2):
            wide = jnp.concatenate([columns[side], columns[side]], axis=1)
            place = pl.ds(0, REACH) if side == 0 else pl.ds(points - REACH, REACH)
            d_ref[p, place, :] = d_ref[p, place, :] + wide * tots[side, one, :]
        top, bottom = pl.ds(0, 1), pl.ds(points - 1, 1)
        d_ref[p, top, :] = d_ref[p, top, :] + tots[2, one, :]
        d_ref[p, bottom, :] = d_ref[p, bottom, :] + tots[3, one, :]
        return carry

    lax.fori_loop(0, planes, correct, 0)

    rows_of(0, n_near, sum_recv).wait()
    shares[1, n_level : n_level + 1, :] = jnp.sum(shares[0], axis=0, keepdims=True)
    for i, there in enumerate(groups[1]):

        @pl.when(jnp.logical_not(skips & (there[0] == first[0]) & (there[1] == first[1])))
        def _(i=i):
            send_sum(1, i).start()

    @pl.when(is_first)
    def _():
        rows_of(1, n_level - n_skip, sum_recv).wait()
        pltpu.make_async_copy(direct, direct, direct_recv).wait()
        extra[...] = jnp.sum(direct[...], axis=0, keepdims=True)

    @pl.when(jnp.logical_not(is_first))
    def _():
        rows_of(1, n_level, sum_recv).wait()

    total = jnp.sum(shares[1], axis=0, keepdims=True) + extra[...]
    count = float(points * ring * 2 * LANES * lax.axis_size("gz"))
    total = total * (1.0 / count)
    per_row = e_ref.shape[1]
    for i in range(e_ref.shape[0]):
        e_ref[i : i + 1, :] = total[:, i * per_row : (i + 1) * per_row]
    rows_of(0, n_near, sum_send).wait()

    @pl.when(skips)
    def _():
        rows_of(1, n_level - 1, sum_send).wait()

    @pl.when(jnp.logical_not(skips))
    def _():
        rows_of(1, n_level, sum_send).wait()

    @pl.when(is_far)
    def _():
        send_direct().wait_send()


def deliver(d_vmem, e_vmem, d_hbm, e_hbm, sem):
    copies = [pltpu.make_async_copy(d_vmem, d_hbm, sem.at[0]), pltpu.make_async_copy(e_vmem, e_hbm, sem.at[1])]
    for copy in copies:
        copy.start()
    for copy in copies:
        copy.wait()


def shards(velocity):
    components, heights, points, spanwise = velocity.shape
    planes = components * heights
    shape = (planes, points, spanwise)
    matrix, columns = tables(points)
    f32, dma = jnp.float32, pltpu.SemaphoreType.DMA
    near, far = pl.BlockSpec(memory_space=pltpu.VMEM), pl.BlockSpec(memory_space=pltpu.HBM)
    halo = (2, components, 2, heights, spanwise)
    group = SIZES["x"] * SIZES["y"]

    derivative, energy = pl.pallas_call(
        derive,
        out_shape=(pltpu.VMEM(shape, f32), pltpu.VMEM((components, heights), f32)),
        in_specs=[far] * 3,
        out_specs=(near,) * 2,
        scratch_shapes=[
            pltpu.VMEM(shape, f32),
            pltpu.VMEM((points, points), f32),
            pltpu.VMEM((points, 3 * points), jnp.bfloat16),
            pltpu.VMEM(columns.shape, f32),
            pltpu.VMEM(halo, f32),
            pltpu.VMEM(halo, f32),
            pltpu.VMEM((7, planes, spanwise), f32),
            pltpu.VMEM((4, planes, spanwise), f32),
            pltpu.VMEM((2, group, LANES), f32),
            dma((planes // PIECE,)),
            dma((2,)),
            dma((2, components)),
            dma((2, components)),
            dma((2,)),
            dma((2,)),
            pltpu.VMEM((len(far_devices()), LANES), f32),
            pltpu.VMEM((1, LANES), f32),
            dma,
            dma,
        ],
        compiler_params=pltpu.CompilerParams(collective_id=0, has_side_effects=True, vmem_limit_bytes=24 * MIB),
        name="derive",
    )(*(
        pltpu.with_memory_space_constraint(operand, pltpu.HBM)
        for operand in (velocity.reshape(shape), jnp.asarray(matrix), jnp.asarray(columns))
    ))
    derivative, energy = pl.pallas_call(
        deliver,
        out_shape=(jax.ShapeDtypeStruct(shape, f32), jax.ShapeDtypeStruct((components, heights), f32)),
        in_specs=[near] * 2,
        out_specs=(far, far),
        scratch_shapes=[dma((2,))],
        compiler_params=pltpu.CompilerParams(vmem_limit_bytes=4 * MIB),
        name="deliver",
    )(derivative, energy)
    return derivative.reshape(velocity.shape), energy


def solution(mesh):
    return jax.shard_map(
        shards,
        mesh=mesh,
        in_specs=(P(None, None, "gx", "gz"),),
        out_specs=(P(None, None, "gx", "gz"), P()),
        check_vma=False,
    )
```

```python
import functools
import itertools
import math

import jax
import jax.numpy as jnp
import numpy as np
from jax import lax
from jax.experimental import pallas as pl
from jax.experimental.pallas import tpu as pltpu
from jax.sharding import PartitionSpec as P

ALPHA = 1.0 / 3.0
HALF_A = 7.0 / 9.0
QUARTER_B = 1.0 / 36.0

ROOT = (math.sqrt(1.0 - 4.0 * ALPHA * ALPHA) - 1.0) / (2.0 * ALPHA)
SCALE = 1.0 / math.sqrt(1.0 - 4.0 * ALPHA * ALPHA)
TAIL = SCALE * (HALF_A + QUARTER_B * (ROOT + 1.0 / ROOT))
CENTRE = SCALE * (HALF_A + 2.0 * QUARTER_B * ROOT)
BUMP = CENTRE - TAIL
REACH = 96

SIZES = {"x": 4, "y": 4, "z": 8, "core": 2}
PHASES = (("x", "y"), ("z", "core"))
AHEAD = {"x": 0, "y": 0, "z": 0, "core": 1}
FAR = range(3, 8)
MESH = pl.DeviceIdType.MESH
LANES = 128
ROW = SIZES["x"] * SIZES["core"]
PIECE = 4
GROUP = 8
MIB = 1024 * 1024


def around():
    gx, gz = lax.axis_index("gx"), lax.axis_index("gz")
    here = {"z": lax.div(gx, 4), "y": lax.rem(gx, 4), "x": lax.div(gz, 2), "core": lax.rem(gz, 2)}

    @functools.cache
    def moved(axis, offset):
        return lax.rem(here[axis] + offset, SIZES[axis]) if offset else here[axis]

    @functools.cache
    def paired(major, minor, one, two):
        if not (one or two):
            return gx if major == "z" else gz
        return moved(major, one) * SIZES[minor] + moved(minor, two)

    def at(x=0, y=0, z=0, core=0):
        return (
            paired("z", "y", z % SIZES["z"], y % SIZES["y"]),
            paired("x", "core", x % SIZES["x"], core % SIZES["core"]),
        )

    return at


def hops(offset, axis):
    return 0 if axis == "core" else min(offset, SIZES[axis] - offset)


def partners(at, axes):
    offsets = [o for o in itertools.product(*(range(SIZES[a]) for a in axes)) if any(o)]
    offsets.sort(key=lambda o: -sum(hops(v, a) for v, a in zip(o, axes)))
    return [at(**dict(zip(axes, offset))) for offset in offsets]


def far_devices():
    found = []
    for z, y, x, core in itertools.product(FAR, *(range(SIZES[a]) for a in ("y", "x", "core"))):
        place = {"x": x, "y": y, "z": z, "core": core}
        away = sum(hops(abs(place[a] - AHEAD[a]), a) for a in place)
        found.append((-away, z * SIZES["y"] + y, x * SIZES["core"] + core))
    return [there for _, *there in sorted(found)]


def tables(points):
    index = np.arange(points)
    distance = np.abs(index[:, None] - index[None, :])
    matrix = np.where(distance == 0, CENTRE, TAIL * ROOT ** distance.astype(np.float64))
    matrix[:, 0] = 0.0
    matrix[:, points - 1] = 0.0
    reach = np.arange(REACH)
    powers = ROOT ** reach.astype(np.float64)
    head = ROOT**reach - ROOT ** (reach + 2.0)
    head[0], head[1] = 0.0, ROOT - ROOT**3
    columns = np.stack([powers, powers[::-1], head, -head[::-1]])
    columns = np.broadcast_to(columns[:, :, None], (4, REACH, LANES))
    return matrix.astype(np.float32), columns.astype(np.float32)


def column_sum(weights, block):
    w = jnp.concatenate([weights, weights], axis=1)
    return jnp.sum(w * block, axis=0, keepdims=True)


def derive(
    v_hbm, matrix_hbm, column_hbm, d_ref, e_ref,
    v, matrix, split, columns, out, got, rows, tots, shares, load_sem, const_sem, halo_send, halo_recv, sum_send, sum_recv,
    direct, extra, direct_send, direct_recv, near_sem, mate_sem,
):
    planes, points, _ = v.shape
    parts, per_part = out.shape[1], out.shape[3]
    gx, gz = lax.axis_index("gx"), lax.axis_index("gz")
    ring = lax.axis_size("gx")
    sides = ((lax.rem(gx + ring - 1, ring), gz), (lax.rem(gx + 1, ring), gz))

    at = around()
    groups = [partners(at, axes) for axes in PHASES]

    shares[1] = jnp.zeros_like(shares[1])
    extra[...] = jnp.zeros_like(extra)

    constants = [
        pltpu.make_async_copy(source, target, const_sem.at[i])
        for i, (source, target) in enumerate(((column_hbm, columns), (matrix_hbm, matrix)))
    ]

    def load(i):
        piece = pl.ds(i * PIECE, PIECE)
        return pltpu.make_async_copy(v_hbm.at[piece], v.at[piece], load_sem.at[i])

    constants[0].start()
    for i in range(planes // PIECE):
        load(i).start()
    constants[1].start()

    def signal(semaphore, there):
        pl.semaphore_signal(semaphore, inc=1, device_id=there, device_id_type=MESH)

    barrier = pltpu.get_barrier_semaphore()
    row, column = partners(at, ("x",)), partners(at, ("y",))
    levels = [at(z=offset) for offset in (2, -2, 1, -1)]
    mate = at(core=1)
    known = list(sides) + levels + row + column + [mate]
    for there in known:
        signal(barrier, there)

    first = (AHEAD["z"] * SIZES["y"] + AHEAD["y"], AHEAD["x"] * SIZES["core"] + AHEAD["core"])
    is_first = (gx == first[0]) & (gz == first[1])
    low, high_end = FAR.start * SIZES["y"], FAR.stop * SIZES["y"]
    is_far = (gx >= low) & (gx < high_end)

    @pl.when(is_first)
    def _():
        for there in far_devices():
            signal(barrier, there)

    constants[0].wait()

    def summarise(part, k):
        p = part * per_part + k
        head, tail = v[p, :REACH, :], v[p, points - REACH :, :]
        first, second = head[0:1], head[1:2]
        last, before = tail[REACH - 1 :], tail[REACH - 2 : REACH - 1]
        one, row = pl.ds(p, 1), pl.ds(k, 1)
        out[0, part, 0, row, :] = first
        out[0, part, 1, row, :] = column_sum(columns[2], head - first)
        out[1, part, 0, row, :] = last
        out[1, part, 1, row, :] = column_sum(columns[3], tail - last)
        rows[0, one, :] = second
        rows[1, one, :] = before

    def halo(part, i):
        return pltpu.make_async_remote_copy(
            src_ref=out.at[i, part], dst_ref=got.at[1 - i, part],
            send_sem=halo_send.at[i, part], recv_sem=halo_recv.at[1 - i, part],
            device_id=sides[i], device_id_type=MESH,
        )

    for part in range(parts):

        def summarise_piece(i, carry):
            load(part * (per_part // PIECE) + i).wait()
            for k in range(PIECE):
                summarise(part, i * PIECE + k)
            return carry

        lax.fori_loop(0, per_part // PIECE, summarise_piece, 0)

    pl.semaphore_wait(barrier, len(known) + is_far.astype(jnp.int32))
    for part in range(parts):
        for i in range(2):
            halo(part, i).start()
    for there in row + levels[:2]:
        signal(near_sem, there)

    constants[1].wait()
    high = matrix[...].astype(jnp.bfloat16)
    split[:, :points] = (matrix[...] - high.astype(jnp.float32)).astype(jnp.bfloat16)
    split[:, points : 2 * points] = high
    split[:, 2 * points :] = high
    def solve(p):
        block = v[p]
        delta = pltpu.roll(block, points - 1, 0) - pltpu.roll(block, 1, 0)
        coarse = delta.astype(jnp.bfloat16)
        fine = (delta - coarse.astype(jnp.float32)).astype(jnp.bfloat16)
        local = jnp.dot(
            split[...], jnp.concatenate([coarse, fine, coarse], axis=0), preferred_element_type=jnp.float32
        )
        d_ref[p] = local
        one = pl.ds(p, 1)
        rows[2, one, :] = local[0:1]
        rows[3, one, :] = local[points - 1 :]
        rows[4, one, :] = column_sum(columns[0], local[:REACH])
        rows[5, one, :] = column_sum(columns[1], local[points - REACH :])
        rows[6, one, :] = jnp.sum(local * local, axis=0, keepdims=True)

    def solve_group(i, carry):
        for k in range(GROUP):
            solve(i * GROUP + k)
        return carry

    lax.fori_loop(0, planes // GROUP, solve_group, 0)

    squares = 1.0 / (1.0 - ROOT * ROOT)
    sums = []
    for part in range(parts):
        span = pl.ds(part * per_part, per_part)
        energy = rows[6, span, :]
        for i in range(2):
            halo(part, i).wait()
        for side, sign in ((0, 1.0), (1, -1.0)):
            own, inner, edge = out[side, part, 0], rows[side, span, :], got[side, part, 0]
            jump = sign * (inner - edge)
            total = jump + got[side, part, 1] + (sign * ROOT) * (own - edge)
            energy = energy + 2.0 * (TAIL * total * rows[4 + side, span, :] + BUMP * jump * rows[2 + side, span, :])
            energy = energy + (TAIL * TAIL * squares) * total * total
            energy = energy + (2.0 * TAIL * BUMP) * total * jump + (BUMP * BUMP) * jump * jump
            tots[side, span, :] = TAIL * total
            tots[2 + side, span, :] = BUMP * jump
        sums.append(jnp.sum(energy[:, :LANES] + energy[:, LANES:], axis=1, keepdims=True))

    chosen = lax.broadcasted_iota(jnp.int32, (planes, LANES), 0) == lax.broadcasted_iota(jnp.int32, (planes, LANES), 1)
    energy = jnp.broadcast_to(jnp.concatenate(sums, axis=0), (planes, LANES))
    share = jnp.sum(jnp.where(chosen, energy, 0.0), axis=0, keepdims=True)

    n_far = direct.shape[0]

    def send_direct():
        return pltpu.make_async_remote_copy(
            src_ref=shares.at[0, pl.ds(len(groups[0]), 1)], dst_ref=direct.at[pl.ds((gx - low) * ROW + gz, 1)],
            send_sem=direct_send, recv_sem=direct_recv, device_id=first, device_id_type=MESH,
        )

    def send_sum(phase, i):
        group = groups[phase]
        return pltpu.make_async_remote_copy(
            src_ref=shares.at[phase, pl.ds(len(group), 1)], dst_ref=shares.at[phase, pl.ds(i, 1)],
            send_sem=sum_send.at[phase], recv_sem=sum_recv.at[phase],
            device_id=group[i], device_id_type=MESH,
        )

    def rows_of(phase, count, semaphore):
        part = shares.at[phase, pl.ds(0, count)]
        return pltpu.make_async_copy(part, part, semaphore.at[phase])

    n_near, n_level = len(groups[0]), len(groups[1])
    skips = is_far & (lax.rem(gx, SIZES["y"]) == AHEAD["y"]) & (lax.div(gz, SIZES["core"]) == AHEAD["x"])
    n_skip = len(FAR) * SIZES["core"]

    shares[0, n_near : n_near + 1, :] = share

    @pl.when(is_far)
    def _():
        send_direct().start()

    pl.semaphore_wait(near_sem, len(row) + 2)
    for i in range(n_near):
        send_sum(0, i).start()

    signal(mate_sem, mate)

    def correct(p, carry):
        one = pl.ds(p, 1)
        for side in range(2):
            wide = jnp.concatenate([columns[side], columns[side]], axis=1)
            place = pl.ds(0, REACH) if side == 0 else pl.ds(points - REACH, REACH)
            d_ref[p, place, :] = d_ref[p, place, :] + wide * tots[side, one, :]
        top, bottom = pl.ds(0, 1), pl.ds(points - 1, 1)
        d_ref[p, top, :] = d_ref[p, top, :] + tots[2, one, :]
        d_ref[p, bottom, :] = d_ref[p, bottom, :] + tots[3, one, :]
        return carry

    lax.fori_loop(0, planes, correct, 0)

    rows_of(0, n_near, sum_recv).wait()
    shares[1, n_level : n_level + 1, :] = jnp.sum(shares[0], axis=0, keepdims=True)
    pl.semaphore_wait(mate_sem, 1)
    for i, there in enumerate(groups[1]):

        @pl.when(jnp.logical_not(skips & (there[0] == first[0]) & (there[1] == first[1])))
        def _(i=i):
            send_sum(1, i).start()

    @pl.when(is_first)
    def _():
        rows_of(1, n_level - n_skip, sum_recv).wait()
        pltpu.make_async_copy(direct, direct, direct_recv).wait()
        extra[...] = jnp.sum(direct[...], axis=0, keepdims=True)

    @pl.when(jnp.logical_not(is_first))
    def _():
        rows_of(1, n_level, sum_recv).wait()

    total = jnp.sum(shares[1], axis=0, keepdims=True) + extra[...]
    count = float(points * ring * 2 * LANES * lax.axis_size("gz"))
    total = total * (1.0 / count)
    per_row = e_ref.shape[1]
    for i in range(e_ref.shape[0]):
        e_ref[i : i + 1, :] = total[:, i * per_row : (i + 1) * per_row]
    rows_of(0, n_near, sum_send).wait()

    @pl.when(skips)
    def _():
        rows_of(1, n_level - 1, sum_send).wait()

    @pl.when(jnp.logical_not(skips))
    def _():
        rows_of(1, n_level, sum_send).wait()

    @pl.when(is_far)
    def _():
        send_direct().wait_send()


def deliver(d_vmem, e_vmem, d_hbm, e_hbm, sem):
    copies = [pltpu.make_async_copy(d_vmem, d_hbm, sem.at[0]), pltpu.make_async_copy(e_vmem, e_hbm, sem.at[1])]
    for copy in copies:
        copy.start()
    for copy in copies:
        copy.wait()


def shards(velocity):
    components, heights, points, spanwise = velocity.shape
    planes = components * heights
    shape = (planes, points, spanwise)
    matrix, columns = tables(points)
    f32, dma = jnp.float32, pltpu.SemaphoreType.DMA
    near, far = pl.BlockSpec(memory_space=pltpu.VMEM), pl.BlockSpec(memory_space=pltpu.HBM)
    halo = (2, components, 2, heights, spanwise)
    group = SIZES["x"] * SIZES["y"]

    derivative, energy = pl.pallas_call(
        derive,
        out_shape=(pltpu.VMEM(shape, f32), pltpu.VMEM((components, heights), f32)),
        in_specs=[far] * 3,
        out_specs=(near,) * 2,
        scratch_shapes=[
            pltpu.VMEM(shape, f32),
            pltpu.VMEM((points, points), f32),
            pltpu.VMEM((points, 3 * points), jnp.bfloat16),
            pltpu.VMEM(columns.shape, f32),
            pltpu.VMEM(halo, f32),
            pltpu.VMEM(halo, f32),
            pltpu.VMEM((7, planes, spanwise), f32),
            pltpu.VMEM((4, planes, spanwise), f32),
            pltpu.VMEM((2, group, LANES), f32),
            dma((planes // PIECE,)),
            dma((2,)),
            dma((2, components)),
            dma((2, components)),
            dma((2,)),
            dma((2,)),
            pltpu.VMEM((len(far_devices()), LANES), f32),
            pltpu.VMEM((1, LANES), f32),
            dma,
            dma,
            pltpu.SemaphoreType.REGULAR,
            pltpu.SemaphoreType.REGULAR,
        ],
        compiler_params=pltpu.CompilerParams(collective_id=0, has_side_effects=True, vmem_limit_bytes=24 * MIB),
        name="derive",
    )(*(
        pltpu.with_memory_space_constraint(operand, pltpu.HBM)
        for operand in (velocity.reshape(shape), jnp.asarray(matrix), jnp.asarray(columns))
    ))
    derivative, energy = pl.pallas_call(
        deliver,
        out_shape=(jax.ShapeDtypeStruct(shape, f32), jax.ShapeDtypeStruct((components, heights), f32)),
        in_specs=[near] * 2,
        out_specs=(far, far),
        scratch_shapes=[dma((2,))],
        compiler_params=pltpu.CompilerParams(vmem_limit_bytes=4 * MIB),
        name="deliver",
    )(derivative, energy)
    return derivative.reshape(velocity.shape), energy


def solution(mesh):
    return jax.shard_map(
        shards,
        mesh=mesh,
        in_specs=(P(None, None, "gx", "gz"),),
        out_specs=(P(None, None, "gx", "gz"), P()),
        check_vma=False,
    )
```

```python
import functools
import itertools
import math

import jax
import jax.numpy as jnp
import numpy as np
from jax import lax
from jax.experimental import pallas as pl
from jax.experimental.pallas import tpu as pltpu
from jax.sharding import PartitionSpec as P

ALPHA = 1.0 / 3.0
HALF_A = 7.0 / 9.0
QUARTER_B = 1.0 / 36.0

ROOT = (math.sqrt(1.0 - 4.0 * ALPHA * ALPHA) - 1.0) / (2.0 * ALPHA)
SCALE = 1.0 / math.sqrt(1.0 - 4.0 * ALPHA * ALPHA)
TAIL = SCALE * (HALF_A + QUARTER_B * (ROOT + 1.0 / ROOT))
CENTRE = SCALE * (HALF_A + 2.0 * QUARTER_B * ROOT)
BUMP = CENTRE - TAIL
REACH = 96

SIZES = {"x": 4, "y": 4, "z": 8, "core": 2}
PHASES = (("x", "y"), ("z", "core"))
AHEAD = {"x": 0, "y": 0, "z": 0, "core": 1}
FAR = range(3, 8)
MESH = pl.DeviceIdType.MESH
LANES = 128
ROW = SIZES["x"] * SIZES["core"]
PIECE = 4
GROUP = 12
MIB = 1024 * 1024


def around():
    gx, gz = lax.axis_index("gx"), lax.axis_index("gz")
    here = {"z": lax.div(gx, 4), "y": lax.rem(gx, 4), "x": lax.div(gz, 2), "core": lax.rem(gz, 2)}

    @functools.cache
    def moved(axis, offset):
        return lax.rem(here[axis] + offset, SIZES[axis]) if offset else here[axis]

    @functools.cache
    def paired(major, minor, one, two):
        if not (one or two):
            return gx if major == "z" else gz
        return moved(major, one) * SIZES[minor] + moved(minor, two)

    def at(x=0, y=0, z=0, core=0):
        return (
            paired("z", "y", z % SIZES["z"], y % SIZES["y"]),
            paired("x", "core", x % SIZES["x"], core % SIZES["core"]),
        )

    return at


def hops(offset, axis):
    return 0 if axis == "core" else min(offset, SIZES[axis] - offset)


def partners(at, axes):
    offsets = [o for o in itertools.product(*(range(SIZES[a]) for a in axes)) if any(o)]
    offsets.sort(key=lambda o: -sum(hops(v, a) for v, a in zip(o, axes)))
    return [at(**dict(zip(axes, offset))) for offset in offsets]


def far_devices():
    found = []
    for z, y, x, core in itertools.product(FAR, *(range(SIZES[a]) for a in ("y", "x", "core"))):
        place = {"x": x, "y": y, "z": z, "core": core}
        away = sum(hops(abs(place[a] - AHEAD[a]), a) for a in place)
        found.append((-away, z * SIZES["y"] + y, x * SIZES["core"] + core))
    return [there for _, *there in sorted(found)]


def tables(points):
    index = np.arange(points)
    distance = np.abs(index[:, None] - index[None, :])
    matrix = np.where(distance == 0, CENTRE, TAIL * ROOT ** distance.astype(np.float64))
    matrix[:, 0] = 0.0
    matrix[:, points - 1] = 0.0
    reach = np.arange(REACH)
    powers = ROOT ** reach.astype(np.float64)
    head = ROOT**reach - ROOT ** (reach + 2.0)
    head[0], head[1] = 0.0, ROOT - ROOT**3
    columns = np.stack([powers, powers[::-1], head, -head[::-1]])
    columns = np.broadcast_to(columns[:, :, None], (4, REACH, LANES))
    return matrix.astype(np.float32), columns.astype(np.float32)


def column_sum(weights, block):
    w = jnp.concatenate([weights, weights], axis=1)
    return jnp.sum(w * block, axis=0, keepdims=True)


def derive(
    v_hbm, matrix_hbm, column_hbm, d_ref, e_ref,
    v, matrix, split, columns, out, got, rows, tots, shares, load_sem, const_sem, halo_send, halo_recv, sum_send, sum_recv,
    direct, extra, direct_send, direct_recv, near_sem, mate_sem,
):
    planes, points, _ = v.shape
    parts, per_part = out.shape[1], out.shape[3]
    gx, gz = lax.axis_index("gx"), lax.axis_index("gz")
    ring = lax.axis_size("gx")
    sides = ((lax.rem(gx + ring - 1, ring), gz), (lax.rem(gx + 1, ring), gz))

    at = around()
    groups = [partners(at, axes) for axes in PHASES]

    shares[1] = jnp.zeros_like(shares[1])
    extra[...] = jnp.zeros_like(extra)

    constants = [
        pltpu.make_async_copy(source, target, const_sem.at[i])
        for i, (source, target) in enumerate(((column_hbm, columns), (matrix_hbm, matrix)))
    ]

    def load(i):
        piece = pl.ds(i * PIECE, PIECE)
        return pltpu.make_async_copy(v_hbm.at[piece], v.at[piece], load_sem.at[i])

    constants[0].start()
    for i in range(planes // PIECE):
        load(i).start()
    constants[1].start()

    def signal(semaphore, there):
        pl.semaphore_signal(semaphore, inc=1, device_id=there, device_id_type=MESH)

    barrier = pltpu.get_barrier_semaphore()
    row, column = partners(at, ("x",)), partners(at, ("y",))
    levels = [at(z=offset) for offset in (2, -2, 1, -1)]
    mate = at(core=1)
    known = [*sides, *levels[:2], row[0], column[0], *levels[2:], *row[1:], *column[1:], mate]
    for there in known:
        signal(barrier, there)

    first = (AHEAD["z"] * SIZES["y"] + AHEAD["y"], AHEAD["x"] * SIZES["core"] + AHEAD["core"])
    is_first = (gx == first[0]) & (gz == first[1])
    low, high_end = FAR.start * SIZES["y"], FAR.stop * SIZES["y"]
    is_far = (gx >= low) & (gx < high_end)

    @pl.when(is_first)
    def _():
        for there in far_devices():
            signal(barrier, there)

    constants[0].wait()

    def summarise(part, k):
        p = part * per_part + k
        head, tail = v[p, :REACH, :], v[p, points - REACH :, :]
        first, second = head[0:1], head[1:2]
        last, before = tail[REACH - 1 :], tail[REACH - 2 : REACH - 1]
        one, row = pl.ds(p, 1), pl.ds(k, 1)
        out[0, part, 0, row, :] = first
        out[0, part, 1, row, :] = column_sum(columns[2], head - first)
        out[1, part, 0, row, :] = last
        out[1, part, 1, row, :] = column_sum(columns[3], tail - last)
        rows[0, one, :] = second
        rows[1, one, :] = before

    def halo(part, i):
        return pltpu.make_async_remote_copy(
            src_ref=out.at[i, part], dst_ref=got.at[1 - i, part],
            send_sem=halo_send.at[i, part], recv_sem=halo_recv.at[1 - i, part],
            device_id=sides[i], device_id_type=MESH,
        )

    for part in range(parts):

        def summarise_piece(i, carry):
            load(part * (per_part // PIECE) + i).wait()
            for k in range(PIECE):
                summarise(part, i * PIECE + k)
            return carry

        lax.fori_loop(0, per_part // PIECE, summarise_piece, 0)
        if part == parts - 2:
            pl.semaphore_wait(barrier, len(known) + is_far.astype(jnp.int32))
        if part >= parts - 2:
            for ready in range(parts - 1) if part == parts - 2 else (part,):
                for i in range(2):
                    halo(ready, i).start()

    for there in row + levels[:2]:
        signal(near_sem, there)

    constants[1].wait()
    high = matrix[...].astype(jnp.bfloat16)
    split[:, :points] = (matrix[...] - high.astype(jnp.float32)).astype(jnp.bfloat16)
    split[:, points : 2 * points] = high
    split[:, 2 * points :] = high
    def solve(p):
        block = v[p]
        delta = pltpu.roll(block, points - 1, 0) - pltpu.roll(block, 1, 0)
        coarse = delta.astype(jnp.bfloat16)
        fine = (delta - coarse.astype(jnp.float32)).astype(jnp.bfloat16)
        local = jnp.dot(
            split[...], jnp.concatenate([coarse, fine, coarse], axis=0), preferred_element_type=jnp.float32
        )
        d_ref[p] = local
        one = pl.ds(p, 1)
        rows[2, one, :] = local[0:1]
        rows[3, one, :] = local[points - 1 :]
        rows[4, one, :] = column_sum(columns[0], local[:REACH])
        rows[5, one, :] = column_sum(columns[1], local[points - REACH :])
        rows[6, one, :] = jnp.sum(local * local, axis=0, keepdims=True)

    def solve_group(i, carry):
        for k in range(GROUP):
            solve(i * GROUP + k)
        return carry

    lax.fori_loop(0, planes // GROUP, solve_group, 0)

    squares = 1.0 / (1.0 - ROOT * ROOT)
    sums = []
    for part in range(parts):
        span = pl.ds(part * per_part, per_part)
        energy = rows[6, span, :]
        for i in range(2):
            halo(part, i).wait()
        for side, sign in ((0, 1.0), (1, -1.0)):
            own, inner, edge = out[side, part, 0], rows[side, span, :], got[side, part, 0]
            jump = sign * (inner - edge)
            total = jump + got[side, part, 1] + (sign * ROOT) * (own - edge)
            energy = energy + 2.0 * (TAIL * total * rows[4 + side, span, :] + BUMP * jump * rows[2 + side, span, :])
            energy = energy + (TAIL * TAIL * squares) * total * total
            energy = energy + (2.0 * TAIL * BUMP) * total * jump + (BUMP * BUMP) * jump * jump
            tots[side, span, :] = TAIL * total
            tots[2 + side, span, :] = BUMP * jump
        sums.append(jnp.sum(energy[:, :LANES] + energy[:, LANES:], axis=1, keepdims=True))

    chosen = lax.broadcasted_iota(jnp.int32, (planes, LANES), 0) == lax.broadcasted_iota(jnp.int32, (planes, LANES), 1)
    energy = jnp.broadcast_to(jnp.concatenate(sums, axis=0), (planes, LANES))
    share = jnp.sum(jnp.where(chosen, energy, 0.0), axis=0, keepdims=True)

    n_far = direct.shape[0]

    def send_direct():
        return pltpu.make_async_remote_copy(
            src_ref=shares.at[0, pl.ds(len(groups[0]), 1)], dst_ref=direct.at[pl.ds((gx - low) * ROW + gz, 1)],
            send_sem=direct_send, recv_sem=direct_recv, device_id=first, device_id_type=MESH,
        )

    def send_sum(phase, i):
        group = groups[phase]
        return pltpu.make_async_remote_copy(
            src_ref=shares.at[phase, pl.ds(len(group), 1)], dst_ref=shares.at[phase, pl.ds(i, 1)],
            send_sem=sum_send.at[phase], recv_sem=sum_recv.at[phase],
            device_id=group[i], device_id_type=MESH,
        )

    def rows_of(phase, count, semaphore):
        part = shares.at[phase, pl.ds(0, count)]
        return pltpu.make_async_copy(part, part, semaphore.at[phase])

    n_near, n_level = len(groups[0]), len(groups[1])
    skips = is_far & (lax.rem(gx, SIZES["y"]) == AHEAD["y"]) & (lax.div(gz, SIZES["core"]) == AHEAD["x"])
    n_skip = len(FAR) * SIZES["core"]

    shares[0, n_near : n_near + 1, :] = share

    @pl.when(is_far)
    def _():
        send_direct().start()

    pl.semaphore_wait(near_sem, len(row) + 2)
    for i in range(n_near):
        send_sum(0, i).start()

    signal(mate_sem, mate)

    def correct(p, carry):
        one = pl.ds(p, 1)
        for side in range(2):
            wide = jnp.concatenate([columns[side], columns[side]], axis=1)
            place = pl.ds(0, REACH) if side == 0 else pl.ds(points - REACH, REACH)
            d_ref[p, place, :] = d_ref[p, place, :] + wide * tots[side, one, :]
        top, bottom = pl.ds(0, 1), pl.ds(points - 1, 1)
        d_ref[p, top, :] = d_ref[p, top, :] + tots[2, one, :]
        d_ref[p, bottom, :] = d_ref[p, bottom, :] + tots[3, one, :]
        return carry

    lax.fori_loop(0, planes, correct, 0)

    rows_of(0, n_near, sum_recv).wait()
    shares[1, n_level : n_level + 1, :] = jnp.sum(shares[0], axis=0, keepdims=True)
    pl.semaphore_wait(mate_sem, 1)
    @pl.when(jnp.logical_not(skips))
    def _():
        for i in range(n_level):
            send_sum(1, i).start()

    @pl.when(skips)
    def _():
        for i, there in enumerate(groups[1]):

            @pl.when(jnp.logical_not((there[0] == first[0]) & (there[1] == first[1])))
            def _(i=i):
                send_sum(1, i).start()

    @pl.when(is_first)
    def _():
        rows_of(1, n_level - n_skip, sum_recv).wait()
        pltpu.make_async_copy(direct, direct, direct_recv).wait()
        extra[...] = jnp.sum(direct[...], axis=0, keepdims=True)

    @pl.when(jnp.logical_not(is_first))
    def _():
        rows_of(1, n_level, sum_recv).wait()

    total = jnp.sum(shares[1], axis=0, keepdims=True) + extra[...]
    count = float(points * ring * 2 * LANES * lax.axis_size("gz"))
    total = total * (1.0 / count)
    per_row = e_ref.shape[1]
    for i in range(e_ref.shape[0]):
        e_ref[i : i + 1, :] = total[:, i * per_row : (i + 1) * per_row]
    rows_of(0, n_near, sum_send).wait()

    @pl.when(skips)
    def _():
        rows_of(1, n_level - 1, sum_send).wait()

    @pl.when(jnp.logical_not(skips))
    def _():
        rows_of(1, n_level, sum_send).wait()

    @pl.when(is_far)
    def _():
        send_direct().wait_send()


def deliver(d_vmem, e_vmem, d_hbm, e_hbm, sem):
    copies = [pltpu.make_async_copy(d_vmem, d_hbm, sem.at[0]), pltpu.make_async_copy(e_vmem, e_hbm, sem.at[1])]
    for copy in copies:
        copy.start()
    for copy in copies:
        copy.wait()


def shards(velocity):
    components, heights, points, spanwise = velocity.shape
    planes = components * heights
    shape = (planes, points, spanwise)
    matrix, columns = tables(points)
    f32, dma = jnp.float32, pltpu.SemaphoreType.DMA
    near, far = pl.BlockSpec(memory_space=pltpu.VMEM), pl.BlockSpec(memory_space=pltpu.HBM)
    halo = (2, components, 2, heights, spanwise)
    group = SIZES["x"] * SIZES["y"]

    derivative, energy = pl.pallas_call(
        derive,
        out_shape=(pltpu.VMEM(shape, f32), pltpu.VMEM((components, heights), f32)),
        in_specs=[far] * 3,
        out_specs=(near,) * 2,
        scratch_shapes=[
            pltpu.VMEM(shape, f32),
            pltpu.VMEM((points, points), f32),
            pltpu.VMEM((points, 3 * points), jnp.bfloat16),
            pltpu.VMEM(columns.shape, f32),
            pltpu.VMEM(halo, f32),
            pltpu.VMEM(halo, f32),
            pltpu.VMEM((7, planes, spanwise), f32),
            pltpu.VMEM((4, planes, spanwise), f32),
            pltpu.VMEM((2, group, LANES), f32),
            dma((planes // PIECE,)),
            dma((2,)),
            dma((2, components)),
            dma((2, components)),
            dma((2,)),
            dma((2,)),
            pltpu.VMEM((len(far_devices()), LANES), f32),
            pltpu.VMEM((1, LANES), f32),
            dma,
            dma,
            pltpu.SemaphoreType.REGULAR,
            pltpu.SemaphoreType.REGULAR,
        ],
        compiler_params=pltpu.CompilerParams(collective_id=0, has_side_effects=True, vmem_limit_bytes=24 * MIB),
        name="derive",
    )(*(
        pltpu.with_memory_space_constraint(operand, pltpu.HBM)
        for operand in (velocity.reshape(shape), jnp.asarray(matrix), jnp.asarray(columns))
    ))
    derivative, energy = pl.pallas_call(
        deliver,
        out_shape=(jax.ShapeDtypeStruct(shape, f32), jax.ShapeDtypeStruct((components, heights), f32)),
        in_specs=[near] * 2,
        out_specs=(far, far),
        scratch_shapes=[dma((2,))],
        compiler_params=pltpu.CompilerParams(vmem_limit_bytes=4 * MIB),
        name="deliver",
    )(derivative, energy)
    return derivative.reshape(velocity.shape), energy


def solution(mesh):
    return jax.shard_map(
        shards,
        mesh=mesh,
        in_specs=(P(None, None, "gx", "gz"),),
        out_specs=(P(None, None, "gx", "gz"), P()),
        check_vma=False,
    )
```

```python
import functools
import itertools
import math

import jax
import jax.numpy as jnp
import numpy as np
from jax import lax
from jax.experimental import pallas as pl
from jax.experimental.pallas import tpu as pltpu
from jax.sharding import PartitionSpec as P

ALPHA = 1.0 / 3.0
HALF_A = 7.0 / 9.0
QUARTER_B = 1.0 / 36.0

ROOT = (math.sqrt(1.0 - 4.0 * ALPHA * ALPHA) - 1.0) / (2.0 * ALPHA)
SCALE = 1.0 / math.sqrt(1.0 - 4.0 * ALPHA * ALPHA)
TAIL = SCALE * (HALF_A + QUARTER_B * (ROOT + 1.0 / ROOT))
CENTRE = SCALE * (HALF_A + 2.0 * QUARTER_B * ROOT)
BUMP = CENTRE - TAIL
REACH = 96

SIZES = {"x": 4, "y": 4, "z": 8, "core": 2}
PHASES = (("x", "y"), ("z", "core"))
AHEAD = (
    (0, 0, 0, 1), (0, 1, 0, 0), (0, 1, 0, 1), (0, 0, 1, 0), (0, 0, 1, 1), (1, 0, 0, 0), (1, 0, 0, 1),
    (0, 2, 0, 0), (0, 2, 0, 1), (0, 3, 0, 0), (0, 3, 0, 1),
)
FAR = range(3, 8)
MESH = pl.DeviceIdType.MESH
LANES = 128
ROW = SIZES["x"] * SIZES["core"]
PIECE = 4
GROUP = 12
MIB = 1024 * 1024


def around():
    gx, gz = lax.axis_index("gx"), lax.axis_index("gz")
    here = {"z": lax.div(gx, 4), "y": lax.rem(gx, 4), "x": lax.div(gz, 2), "core": lax.rem(gz, 2)}

    @functools.cache
    def moved(axis, offset):
        return lax.rem(here[axis] + offset, SIZES[axis]) if offset else here[axis]

    @functools.cache
    def paired(major, minor, one, two):
        if not (one or two):
            return gx if major == "z" else gz
        return moved(major, one) * SIZES[minor] + moved(minor, two)

    def at(x=0, y=0, z=0, core=0):
        return (
            paired("z", "y", z % SIZES["z"], y % SIZES["y"]),
            paired("x", "core", x % SIZES["x"], core % SIZES["core"]),
        )

    return at


def hops(offset, axis):
    return 0 if axis == "core" else min(offset, SIZES[axis] - offset)


def partners(at, axes):
    offsets = [o for o in itertools.product(*(range(SIZES[a]) for a in axes)) if any(o)]
    offsets.sort(key=lambda o: -sum(hops(v, a) for v, a in zip(o, axes)))
    return [at(**dict(zip(axes, offset))) for offset in offsets]


def place_of(x, y, z, core):
    return z * SIZES["y"] + y, x * SIZES["core"] + core


def far_devices(x=0, y=0, z=0, core=0):
    found = []
    for there in itertools.product(*(range(SIZES[a]) for a in ("x", "y")), FAR, range(SIZES["core"])):
        away = sum(hops(abs(to - at), a) for to, at, a in zip(there, (x, y, z, core), ("x", "y", "z", "core")))
        found.append((-away, *place_of(*there)))
    return [tuple(there) for _, *there in sorted(found)]


def tables(points):
    index = np.arange(points)
    distance = np.abs(index[:, None] - index[None, :])
    matrix = np.where(distance == 0, CENTRE, TAIL * ROOT ** distance.astype(np.float64))
    matrix[:, 0] = 0.0
    matrix[:, points - 1] = 0.0
    reach = np.arange(REACH)
    powers = ROOT ** reach.astype(np.float64)
    head = ROOT**reach - ROOT ** (reach + 2.0)
    head[0], head[1] = 0.0, ROOT - ROOT**3
    columns = np.stack([powers, powers[::-1], head, -head[::-1]])
    columns = np.broadcast_to(columns[:, :, None], (4, REACH, LANES))
    return matrix.astype(np.float32), columns.astype(np.float32)


def column_sum(weights, block):
    w = jnp.concatenate([weights, weights], axis=1)
    return jnp.sum(w * block, axis=0, keepdims=True)


def derive(
    v_hbm, matrix_hbm, column_hbm, d_ref, e_ref,
    v, matrix, split, columns, out, got, rows, tots, shares, load_sem, const_sem, halo_send, halo_recv, sum_send, sum_recv,
    direct, extra, direct_send, direct_recv, near_sem, mate_sem,
):
    planes, points, _ = v.shape
    parts, per_part = out.shape[1], out.shape[3]
    gx, gz = lax.axis_index("gx"), lax.axis_index("gz")
    ring = lax.axis_size("gx")
    sides = ((lax.rem(gx + ring - 1, ring), gz), (lax.rem(gx + 1, ring), gz))

    at = around()
    groups = [partners(at, axes) for axes in PHASES]

    shares[1] = jnp.zeros_like(shares[1])
    extra[...] = jnp.zeros_like(extra)

    constants = [
        pltpu.make_async_copy(source, target, const_sem.at[i])
        for i, (source, target) in enumerate(((column_hbm, columns), (matrix_hbm, matrix)))
    ]

    def load(i):
        piece = pl.ds(i * PIECE, PIECE)
        return pltpu.make_async_copy(v_hbm.at[piece], v.at[piece], load_sem.at[i])

    constants[0].start()
    for i in range(planes // PIECE):
        load(i).start()
    constants[1].start()

    def signal(semaphore, there):
        pl.semaphore_signal(semaphore, inc=1, device_id=there, device_id_type=MESH)

    barrier = pltpu.get_barrier_semaphore()
    row, column = partners(at, ("x",)), partners(at, ("y",))
    levels = [at(z=offset) for offset in (2, -2, 1, -1)]
    mate = at(core=1)
    known = [*sides, *levels[:2], row[0], column[0], *levels[2:], *row[1:], *column[1:], mate]
    for there in known:
        signal(barrier, there)

    ahead = [place_of(*there) for there in AHEAD]
    is_ahead = functools.reduce(jnp.logical_or, ((gx == there[0]) & (gz == there[1]) for there in ahead))
    low, high_end = FAR.start * SIZES["y"], FAR.stop * SIZES["y"]
    is_far = (gx >= low) & (gx < high_end)

    for place, there in zip(AHEAD, ahead):

        @pl.when((gx == there[0]) & (gz == there[1]))
        def _(place=place):
            for target in far_devices(*place):
                signal(barrier, target)

    constants[0].wait()

    def summarise(part, k):
        p = part * per_part + k
        head, tail = v[p, :REACH, :], v[p, points - REACH :, :]
        first, second = head[0:1], head[1:2]
        last, before = tail[REACH - 1 :], tail[REACH - 2 : REACH - 1]
        one, row = pl.ds(p, 1), pl.ds(k, 1)
        out[0, part, 0, row, :] = first
        out[0, part, 1, row, :] = column_sum(columns[2], head - first)
        out[1, part, 0, row, :] = last
        out[1, part, 1, row, :] = column_sum(columns[3], tail - last)
        rows[0, one, :] = second
        rows[1, one, :] = before

    def halo(part, i):
        return pltpu.make_async_remote_copy(
            src_ref=out.at[i, part], dst_ref=got.at[1 - i, part],
            send_sem=halo_send.at[i, part], recv_sem=halo_recv.at[1 - i, part],
            device_id=sides[i], device_id_type=MESH,
        )

    for part in range(parts):

        def summarise_piece(i, carry):
            load(part * (per_part // PIECE) + i).wait()
            for k in range(PIECE):
                summarise(part, i * PIECE + k)
            return carry

        lax.fori_loop(0, per_part // PIECE, summarise_piece, 0)
        if part == parts - 2:
            pl.semaphore_wait(barrier, len(known) + len(AHEAD) * is_far.astype(jnp.int32))
        if part >= parts - 2:
            for ready in range(parts - 1) if part == parts - 2 else (part,):
                for i in range(2):
                    halo(ready, i).start()

    for there in row + levels[:2]:
        signal(near_sem, there)

    constants[1].wait()
    high = matrix[...].astype(jnp.bfloat16)
    split[:, :points] = (matrix[...] - high.astype(jnp.float32)).astype(jnp.bfloat16)
    split[:, points : 2 * points] = high
    split[:, 2 * points :] = high
    def solve(p):
        block = v[p]
        delta = pltpu.roll(block, points - 1, 0) - pltpu.roll(block, 1, 0)
        coarse = delta.astype(jnp.bfloat16)
        fine = (delta - coarse.astype(jnp.float32)).astype(jnp.bfloat16)
        local = jnp.dot(
            split[...], jnp.concatenate([coarse, fine, coarse], axis=0), preferred_element_type=jnp.float32
        )
        d_ref[p] = local
        one = pl.ds(p, 1)
        rows[2, one, :] = local[0:1]
        rows[3, one, :] = local[points - 1 :]
        rows[4, one, :] = column_sum(columns[0], local[:REACH])
        rows[5, one, :] = column_sum(columns[1], local[points - REACH :])
        rows[6, one, :] = jnp.sum(local * local, axis=0, keepdims=True)

    def solve_group(i, carry):
        for k in range(GROUP):
            solve(i * GROUP + k)
        return carry

    lax.fori_loop(0, planes // GROUP, solve_group, 0)

    squares = 1.0 / (1.0 - ROOT * ROOT)
    sums = []
    for part in range(parts):
        span = pl.ds(part * per_part, per_part)
        energy = rows[6, span, :]
        for i in range(2):
            halo(part, i).wait()
        for side, sign in ((0, 1.0), (1, -1.0)):
            own, inner, edge = out[side, part, 0], rows[side, span, :], got[side, part, 0]
            jump = sign * (inner - edge)
            total = jump + got[side, part, 1] + (sign * ROOT) * (own - edge)
            energy = energy + 2.0 * (TAIL * total * rows[4 + side, span, :] + BUMP * jump * rows[2 + side, span, :])
            energy = energy + (TAIL * TAIL * squares) * total * total
            energy = energy + (2.0 * TAIL * BUMP) * total * jump + (BUMP * BUMP) * jump * jump
            tots[side, span, :] = TAIL * total
            tots[2 + side, span, :] = BUMP * jump
        sums.append(jnp.sum(energy[:, :LANES] + energy[:, LANES:], axis=1, keepdims=True))

    chosen = lax.broadcasted_iota(jnp.int32, (planes, LANES), 0) == lax.broadcasted_iota(jnp.int32, (planes, LANES), 1)
    energy = jnp.broadcast_to(jnp.concatenate(sums, axis=0), (planes, LANES))
    share = jnp.sum(jnp.where(chosen, energy, 0.0), axis=0, keepdims=True)

    n_far = direct.shape[0]

    def send_direct(target):
        return pltpu.make_async_remote_copy(
            src_ref=shares.at[0, pl.ds(len(groups[0]), 1)], dst_ref=direct.at[pl.ds((gx - low) * ROW + gz, 1)],
            send_sem=direct_send, recv_sem=direct_recv, device_id=target, device_id_type=MESH,
        )

    def send_sum(phase, i):
        group = groups[phase]
        return pltpu.make_async_remote_copy(
            src_ref=shares.at[phase, pl.ds(len(group), 1)], dst_ref=shares.at[phase, pl.ds(i, 1)],
            send_sem=sum_send.at[phase], recv_sem=sum_recv.at[phase],
            device_id=group[i], device_id_type=MESH,
        )

    def rows_of(phase, count, semaphore):
        part = shares.at[phase, pl.ds(0, count)]
        return pltpu.make_async_copy(part, part, semaphore.at[phase])

    n_near, n_level = len(groups[0]), len(groups[1])
    skips = {}
    for x, y, _, _ in AHEAD:
        skips.setdefault((x, y), sum(place[:2] == (x, y) for place in AHEAD))
    here = lax.rem(gx, SIZES["y"]), lax.div(gz, SIZES["core"])
    skip = {xy: is_far & (here[0] == xy[1]) & (here[1] == xy[0]) for xy in skips}
    skips_none = jnp.logical_not(functools.reduce(jnp.logical_or, skip.values()))
    n_skip = len(FAR) * SIZES["core"]

    shares[0, n_near : n_near + 1, :] = share

    @pl.when(is_far)
    def _():
        send_direct(ahead[0]).start()

    pl.semaphore_wait(near_sem, len(row) + 2)
    for i in range(n_near):
        send_sum(0, i).start()

    @pl.when(is_far)
    def _():
        for target in ahead[1:]:
            send_direct(target).start()

    signal(mate_sem, mate)

    def correct(p, carry):
        one = pl.ds(p, 1)
        for side in range(2):
            wide = jnp.concatenate([columns[side], columns[side]], axis=1)
            place = pl.ds(0, REACH) if side == 0 else pl.ds(points - REACH, REACH)
            d_ref[p, place, :] = d_ref[p, place, :] + wide * tots[side, one, :]
        top, bottom = pl.ds(0, 1), pl.ds(points - 1, 1)
        d_ref[p, top, :] = d_ref[p, top, :] + tots[2, one, :]
        d_ref[p, bottom, :] = d_ref[p, bottom, :] + tots[3, one, :]
        return carry

    lax.fori_loop(0, planes, correct, 0)

    rows_of(0, n_near, sum_recv).wait()
    shares[1, n_level : n_level + 1, :] = jnp.sum(shares[0], axis=0, keepdims=True)
    pl.semaphore_wait(mate_sem, 1)
    @pl.when(skips_none)
    def _():
        for i in range(n_level):
            send_sum(1, i).start()

    for xy, condition in skip.items():

        @pl.when(condition)
        def _(xy=xy):
            kept = [there for place, there in zip(AHEAD, ahead) if place[:2] == xy]
            for i, there in enumerate(groups[1]):
                spared = functools.reduce(jnp.logical_or, ((there[0] == k[0]) & (there[1] == k[1]) for k in kept))

                @pl.when(jnp.logical_not(spared))
                def _(i=i):
                    send_sum(1, i).start()

    @pl.when(is_ahead)
    def _():
        rows_of(1, n_level - n_skip, sum_recv).wait()
        pltpu.make_async_copy(direct, direct, direct_recv).wait()
        extra[...] = jnp.sum(direct[...], axis=0, keepdims=True)

    @pl.when(jnp.logical_not(is_ahead))
    def _():
        rows_of(1, n_level, sum_recv).wait()

    total = jnp.sum(shares[1], axis=0, keepdims=True) + extra[...]
    count = float(points * ring * 2 * LANES * lax.axis_size("gz"))
    total = total * (1.0 / count)
    per_row = e_ref.shape[1]
    for i in range(e_ref.shape[0]):
        e_ref[i : i + 1, :] = total[:, i * per_row : (i + 1) * per_row]
    rows_of(0, n_near, sum_send).wait()

    @pl.when(skips_none)
    def _():
        rows_of(1, n_level, sum_send).wait()

    for xy, condition in skip.items():

        @pl.when(condition)
        def _(xy=xy):
            rows_of(1, n_level - skips[xy], sum_send).wait()

    @pl.when(is_far)
    def _():
        part = direct.at[pl.ds(0, len(ahead))]
        pltpu.make_async_copy(part, part, direct_send).wait()


def deliver(d_vmem, e_vmem, d_hbm, e_hbm, sem):
    copies = [pltpu.make_async_copy(d_vmem, d_hbm, sem.at[0]), pltpu.make_async_copy(e_vmem, e_hbm, sem.at[1])]
    for copy in copies:
        copy.start()
    for copy in copies:
        copy.wait()


def shards(velocity):
    components, heights, points, spanwise = velocity.shape
    planes = components * heights
    shape = (planes, points, spanwise)
    matrix, columns = tables(points)
    f32, dma = jnp.float32, pltpu.SemaphoreType.DMA
    near, far = pl.BlockSpec(memory_space=pltpu.VMEM), pl.BlockSpec(memory_space=pltpu.HBM)
    halo = (2, components, 2, heights, spanwise)
    group = SIZES["x"] * SIZES["y"]

    derivative, energy = pl.pallas_call(
        derive,
        out_shape=(pltpu.VMEM(shape, f32), pltpu.VMEM((components, heights), f32)),
        in_specs=[far] * 3,
        out_specs=(near,) * 2,
        scratch_shapes=[
            pltpu.VMEM(shape, f32),
            pltpu.VMEM((points, points), f32),
            pltpu.VMEM((points, 3 * points), jnp.bfloat16),
            pltpu.VMEM(columns.shape, f32),
            pltpu.VMEM(halo, f32),
            pltpu.VMEM(halo, f32),
            pltpu.VMEM((7, planes, spanwise), f32),
            pltpu.VMEM((4, planes, spanwise), f32),
            pltpu.VMEM((2, group, LANES), f32),
            dma((planes // PIECE,)),
            dma((2,)),
            dma((2, components)),
            dma((2, components)),
            dma((2,)),
            dma((2,)),
            pltpu.VMEM((len(far_devices()), LANES), f32),
            pltpu.VMEM((1, LANES), f32),
            dma,
            dma,
            pltpu.SemaphoreType.REGULAR,
            pltpu.SemaphoreType.REGULAR,
        ],
        compiler_params=pltpu.CompilerParams(collective_id=0, has_side_effects=True, vmem_limit_bytes=24 * MIB),
        name="derive",
    )(*(
        pltpu.with_memory_space_constraint(operand, pltpu.HBM)
        for operand in (velocity.reshape(shape), jnp.asarray(matrix), jnp.asarray(columns))
    ))
    derivative, energy = pl.pallas_call(
        deliver,
        out_shape=(jax.ShapeDtypeStruct(shape, f32), jax.ShapeDtypeStruct((components, heights), f32)),
        in_specs=[near] * 2,
        out_specs=(far, far),
        scratch_shapes=[dma((2,))],
        compiler_params=pltpu.CompilerParams(vmem_limit_bytes=4 * MIB),
        name="deliver",
    )(derivative, energy)
    return derivative.reshape(velocity.shape), energy


def solution(mesh):
    return jax.shard_map(
        shards,
        mesh=mesh,
        in_specs=(P(None, None, "gx", "gz"),),
        out_specs=(P(None, None, "gx", "gz"), P()),
        check_vma=False,
    )
```

```python
import functools
import itertools
import math

import jax
import jax.numpy as jnp
import numpy as np
from jax import lax
from jax.experimental import pallas as pl
from jax.experimental.pallas import tpu as pltpu
from jax.sharding import PartitionSpec as P

ALPHA = 1.0 / 3.0
HALF_A = 7.0 / 9.0
QUARTER_B = 1.0 / 36.0

ROOT = (math.sqrt(1.0 - 4.0 * ALPHA * ALPHA) - 1.0) / (2.0 * ALPHA)
SCALE = 1.0 / math.sqrt(1.0 - 4.0 * ALPHA * ALPHA)
TAIL = SCALE * (HALF_A + QUARTER_B * (ROOT + 1.0 / ROOT))
CENTRE = SCALE * (HALF_A + 2.0 * QUARTER_B * ROOT)
BUMP = CENTRE - TAIL
REACH = 96

SIZES = {"x": 4, "y": 4, "z": 8, "core": 2}
PHASES = (("x", "y"), ("z", "core"))
AHEAD = (
    (0, 0, 0, 1), (0, 1, 0, 0), (0, 1, 0, 1), (0, 0, 1, 0), (0, 0, 1, 1), (1, 0, 0, 0), (1, 0, 0, 1),
    (0, 2, 0, 0), (0, 2, 0, 1), (0, 3, 0, 0), (0, 3, 0, 1), (0, 0, 2, 0), (0, 0, 2, 1),
    (0, 1, 1, 0), (0, 1, 1, 1), (1, 0, 1, 0), (1, 0, 1, 1),
)
FAR = range(3, 8)
MESH = pl.DeviceIdType.MESH
LANES = 128
ROW = SIZES["x"] * SIZES["core"]
PIECE = 4
GROUP = 12
MIB = 1024 * 1024


def around():
    gx, gz = lax.axis_index("gx"), lax.axis_index("gz")
    here = {"z": lax.div(gx, 4), "y": lax.rem(gx, 4), "x": lax.div(gz, 2), "core": lax.rem(gz, 2)}

    @functools.cache
    def moved(axis, offset):
        return lax.rem(here[axis] + offset, SIZES[axis]) if offset else here[axis]

    @functools.cache
    def paired(major, minor, one, two):
        if not (one or two):
            return gx if major == "z" else gz
        return moved(major, one) * SIZES[minor] + moved(minor, two)

    def at(x=0, y=0, z=0, core=0):
        return (
            paired("z", "y", z % SIZES["z"], y % SIZES["y"]),
            paired("x", "core", x % SIZES["x"], core % SIZES["core"]),
        )

    return at


def hops(offset, axis):
    return 0 if axis == "core" else min(offset, SIZES[axis] - offset)


def partners(at, axes):
    offsets = [o for o in itertools.product(*(range(SIZES[a]) for a in axes)) if any(o)]
    offsets.sort(key=lambda o: -sum(hops(v, a) for v, a in zip(o, axes)))
    return [at(**dict(zip(axes, offset))) for offset in offsets]


def place_of(x, y, z, core):
    return z * SIZES["y"] + y, x * SIZES["core"] + core


def far_devices(x=0, y=0):
    found = []
    for there in itertools.product(*(range(SIZES[a]) for a in ("x", "y")), FAR, range(SIZES["core"])):
        away = sum(hops(abs(to - at), a) for to, at, a in zip(there, (x, y), ("x", "y")))
        found.append((there[2], away, *place_of(*there)))
    return [tuple(there) for _, _, *there in sorted(found)]


def tables(points):
    index = np.arange(points)
    distance = np.abs(index[:, None] - index[None, :])
    matrix = np.where(distance == 0, CENTRE, TAIL * ROOT ** distance.astype(np.float64))
    matrix[:, 0] = 0.0
    matrix[:, points - 1] = 0.0
    reach = np.arange(REACH)
    powers = ROOT ** reach.astype(np.float64)
    head = ROOT**reach - ROOT ** (reach + 2.0)
    head[0], head[1] = 0.0, ROOT - ROOT**3
    columns = np.stack([powers, powers[::-1], head, -head[::-1]])
    columns = np.broadcast_to(columns[:, :, None], (4, REACH, LANES))
    return matrix.astype(np.float32), columns.astype(np.float32)


def column_sum(weights, block):
    w = jnp.concatenate([weights, weights], axis=1)
    return jnp.sum(w * block, axis=0, keepdims=True)


def derive(
    v_hbm, matrix_hbm, column_hbm, d_ref, e_ref,
    v, matrix, split, columns, out, got, rows, tots, shares, load_sem, const_sem, halo_send, halo_recv, sum_send, sum_recv,
    direct, extra, direct_send, direct_recv, near_sem, mate_sem,
):
    planes, points, _ = v.shape
    parts, per_part = out.shape[1], out.shape[3]
    gx, gz = lax.axis_index("gx"), lax.axis_index("gz")
    ring = lax.axis_size("gx")
    sides = ((lax.rem(gx + ring - 1, ring), gz), (lax.rem(gx + 1, ring), gz))

    at = around()
    groups = [partners(at, axes) for axes in PHASES]

    shares[1] = jnp.zeros_like(shares[1])
    extra[...] = jnp.zeros_like(extra)

    constants = [
        pltpu.make_async_copy(source, target, const_sem.at[i])
        for i, (source, target) in enumerate(((column_hbm, columns), (matrix_hbm, matrix)))
    ]

    def load(i):
        piece = pl.ds(i * PIECE, PIECE)
        return pltpu.make_async_copy(v_hbm.at[piece], v.at[piece], load_sem.at[i])

    constants[0].start()
    for i in range(planes // PIECE):
        load(i).start()
    constants[1].start()

    def signal(semaphore, there):
        pl.semaphore_signal(semaphore, inc=1, device_id=there, device_id_type=MESH)

    barrier = pltpu.get_barrier_semaphore()
    row, column = partners(at, ("x",)), partners(at, ("y",))
    levels = [at(z=offset) for offset in (2, -2, 1, -1)]
    mate = at(core=1)
    known = [*sides, *levels[:2], row[0], column[0], *levels[2:], *row[1:], *column[1:], mate]
    for there in known:
        signal(barrier, there)

    ahead = [place_of(*there) for there in AHEAD]
    is_ahead = functools.reduce(jnp.logical_or, ((gx == there[0]) & (gz == there[1]) for there in ahead))
    low, high_end = FAR.start * SIZES["y"], FAR.stop * SIZES["y"]
    is_far = (gx >= low) & (gx < high_end)

    for place, there in zip(AHEAD, ahead):

        @pl.when((gx == there[0]) & (gz == there[1]))
        def _(place=place):
            for target in far_devices(*place[:2]):
                signal(barrier, target)

    constants[0].wait()

    def summarise(part, k):
        p = part * per_part + k
        head, tail = v[p, :REACH, :], v[p, points - REACH :, :]
        first, second = head[0:1], head[1:2]
        last, before = tail[REACH - 1 :], tail[REACH - 2 : REACH - 1]
        one, row = pl.ds(p, 1), pl.ds(k, 1)
        out[0, part, 0, row, :] = first
        out[0, part, 1, row, :] = column_sum(columns[2], head - first)
        out[1, part, 0, row, :] = last
        out[1, part, 1, row, :] = column_sum(columns[3], tail - last)
        rows[0, one, :] = second
        rows[1, one, :] = before

    def halo(part, i):
        return pltpu.make_async_remote_copy(
            src_ref=out.at[i, part], dst_ref=got.at[1 - i, part],
            send_sem=halo_send.at[i, part], recv_sem=halo_recv.at[1 - i, part],
            device_id=sides[i], device_id_type=MESH,
        )

    for part in range(parts):

        def summarise_piece(i, carry):
            load(part * (per_part // PIECE) + i).wait()
            for k in range(PIECE):
                summarise(part, i * PIECE + k)
            return carry

        lax.fori_loop(0, per_part // PIECE, summarise_piece, 0)
        if part == parts - 2:
            pl.semaphore_wait(barrier, len(known) + len(AHEAD) * is_far.astype(jnp.int32))
        if part >= parts - 2:
            for ready in range(parts - 1) if part == parts - 2 else (part,):
                for i in range(2):
                    halo(ready, i).start()

    for there in row + levels[:2]:
        signal(near_sem, there)

    constants[1].wait()
    high = matrix[...].astype(jnp.bfloat16)
    split[:, :points] = (matrix[...] - high.astype(jnp.float32)).astype(jnp.bfloat16)
    split[:, points : 2 * points] = high
    split[:, 2 * points :] = high
    def solve(p):
        block = v[p]
        delta = pltpu.roll(block, points - 1, 0) - pltpu.roll(block, 1, 0)
        coarse = delta.astype(jnp.bfloat16)
        fine = (delta - coarse.astype(jnp.float32)).astype(jnp.bfloat16)
        local = jnp.dot(
            split[...], jnp.concatenate([coarse, fine, coarse], axis=0), preferred_element_type=jnp.float32
        )
        d_ref[p] = local
        one = pl.ds(p, 1)
        rows[2, one, :] = local[0:1]
        rows[3, one, :] = local[points - 1 :]
        rows[4, one, :] = column_sum(columns[0], local[:REACH])
        rows[5, one, :] = column_sum(columns[1], local[points - REACH :])
        rows[6, one, :] = jnp.sum(local * local, axis=0, keepdims=True)

    def solve_group(i, carry):
        for k in range(GROUP):
            solve(i * GROUP + k)
        return carry

    lax.fori_loop(0, planes // GROUP, solve_group, 0)

    squares = 1.0 / (1.0 - ROOT * ROOT)
    sums = []
    for part in range(parts):
        span = pl.ds(part * per_part, per_part)
        energy = rows[6, span, :]
        for i in range(2):
            halo(part, i).wait()
        for side, sign in ((0, 1.0), (1, -1.0)):
            own, inner, edge = out[side, part, 0], rows[side, span, :], got[side, part, 0]
            jump = sign * (inner - edge)
            total = jump + got[side, part, 1] + (sign * ROOT) * (own - edge)
            energy = energy + 2.0 * (TAIL * total * rows[4 + side, span, :] + BUMP * jump * rows[2 + side, span, :])
            energy = energy + (TAIL * TAIL * squares) * total * total
            energy = energy + (2.0 * TAIL * BUMP) * total * jump + (BUMP * BUMP) * jump * jump
            tots[side, span, :] = TAIL * total
            tots[2 + side, span, :] = BUMP * jump
        sums.append(jnp.sum(energy[:, :LANES] + energy[:, LANES:], axis=1, keepdims=True))

    chosen = lax.broadcasted_iota(jnp.int32, (planes, LANES), 0) == lax.broadcasted_iota(jnp.int32, (planes, LANES), 1)
    energy = jnp.broadcast_to(jnp.concatenate(sums, axis=0), (planes, LANES))
    share = jnp.sum(jnp.where(chosen, energy, 0.0), axis=0, keepdims=True)

    n_far = direct.shape[0]

    def send_direct(target):
        return pltpu.make_async_remote_copy(
            src_ref=shares.at[0, pl.ds(len(groups[0]), 1)], dst_ref=direct.at[pl.ds((gx - low) * ROW + gz, 1)],
            send_sem=direct_send, recv_sem=direct_recv, device_id=target, device_id_type=MESH,
        )

    def send_sum(phase, i):
        group = groups[phase]
        return pltpu.make_async_remote_copy(
            src_ref=shares.at[phase, pl.ds(len(group), 1)], dst_ref=shares.at[phase, pl.ds(i, 1)],
            send_sem=sum_send.at[phase], recv_sem=sum_recv.at[phase],
            device_id=group[i], device_id_type=MESH,
        )

    def rows_of(phase, count, semaphore):
        part = shares.at[phase, pl.ds(0, count)]
        return pltpu.make_async_copy(part, part, semaphore.at[phase])

    n_near, n_level = len(groups[0]), len(groups[1])
    skips = {}
    for x, y, _, _ in AHEAD:
        skips.setdefault((x, y), sum(place[:2] == (x, y) for place in AHEAD))
    here = lax.rem(gx, SIZES["y"]), lax.div(gz, SIZES["core"])
    skip = {xy: is_far & (here[0] == xy[1]) & (here[1] == xy[0]) for xy in skips}
    skips_none = jnp.logical_not(functools.reduce(jnp.logical_or, skip.values()))
    n_skip = len(FAR) * SIZES["core"]

    shares[0, n_near : n_near + 1, :] = share

    @pl.when(is_far)
    def _():
        send_direct(ahead[0]).start()

    pl.semaphore_wait(near_sem, len(row) + 2)
    for i in range(n_near):
        send_sum(0, i).start()

    @pl.when(is_far)
    def _():
        for target in ahead[1:]:
            send_direct(target).start()

    signal(mate_sem, mate)

    def correct(p, carry):
        one = pl.ds(p, 1)
        for side in range(2):
            wide = jnp.concatenate([columns[side], columns[side]], axis=1)
            place = pl.ds(0, REACH) if side == 0 else pl.ds(points - REACH, REACH)
            d_ref[p, place, :] = d_ref[p, place, :] + wide * tots[side, one, :]
        top, bottom = pl.ds(0, 1), pl.ds(points - 1, 1)
        d_ref[p, top, :] = d_ref[p, top, :] + tots[2, one, :]
        d_ref[p, bottom, :] = d_ref[p, bottom, :] + tots[3, one, :]
        return carry

    lax.fori_loop(0, planes, correct, 0)

    rows_of(0, n_near, sum_recv).wait()
    shares[1, n_level : n_level + 1, :] = jnp.sum(shares[0], axis=0, keepdims=True)
    pl.semaphore_wait(mate_sem, 1)
    @pl.when(skips_none)
    def _():
        for i in range(n_level):
            send_sum(1, i).start()

    for xy, condition in skip.items():

        @pl.when(condition)
        def _(xy=xy):
            kept = [there for place, there in zip(AHEAD, ahead) if place[:2] == xy]
            for i, there in enumerate(groups[1]):
                spared = functools.reduce(jnp.logical_or, ((there[0] == k[0]) & (there[1] == k[1]) for k in kept))

                @pl.when(jnp.logical_not(spared))
                def _(i=i):
                    send_sum(1, i).start()

    @pl.when(is_ahead)
    def _():
        rows_of(1, n_level - n_skip, sum_recv).wait()
        pltpu.make_async_copy(direct, direct, direct_recv).wait()
        extra[...] = jnp.sum(direct[...], axis=0, keepdims=True)

    @pl.when(jnp.logical_not(is_ahead))
    def _():
        rows_of(1, n_level, sum_recv).wait()

    total = jnp.sum(shares[1], axis=0, keepdims=True) + extra[...]
    count = float(points * ring * 2 * LANES * lax.axis_size("gz"))
    total = total * (1.0 / count)
    per_row = e_ref.shape[1]
    for i in range(e_ref.shape[0]):
        e_ref[i : i + 1, :] = total[:, i * per_row : (i + 1) * per_row]
    rows_of(0, n_near, sum_send).wait()

    @pl.when(skips_none)
    def _():
        rows_of(1, n_level, sum_send).wait()

    for xy, condition in skip.items():

        @pl.when(condition)
        def _(xy=xy):
            rows_of(1, n_level - skips[xy], sum_send).wait()

    @pl.when(is_far)
    def _():
        part = direct.at[pl.ds(0, len(ahead))]
        pltpu.make_async_copy(part, part, direct_send).wait()


def deliver(d_vmem, e_vmem, d_hbm, e_hbm, sem):
    copies = [pltpu.make_async_copy(d_vmem, d_hbm, sem.at[0]), pltpu.make_async_copy(e_vmem, e_hbm, sem.at[1])]
    for copy in copies:
        copy.start()
    for copy in copies:
        copy.wait()


def shards(velocity):
    components, heights, points, spanwise = velocity.shape
    planes = components * heights
    shape = (planes, points, spanwise)
    matrix, columns = tables(points)
    f32, dma = jnp.float32, pltpu.SemaphoreType.DMA
    near, far = pl.BlockSpec(memory_space=pltpu.VMEM), pl.BlockSpec(memory_space=pltpu.HBM)
    halo = (2, components, 2, heights, spanwise)
    group = SIZES["x"] * SIZES["y"]

    derivative, energy = pl.pallas_call(
        derive,
        out_shape=(pltpu.VMEM(shape, f32), pltpu.VMEM((components, heights), f32)),
        in_specs=[far] * 3,
        out_specs=(near,) * 2,
        scratch_shapes=[
            pltpu.VMEM(shape, f32),
            pltpu.VMEM((points, points), f32),
            pltpu.VMEM((points, 3 * points), jnp.bfloat16),
            pltpu.VMEM(columns.shape, f32),
            pltpu.VMEM(halo, f32),
            pltpu.VMEM(halo, f32),
            pltpu.VMEM((7, planes, spanwise), f32),
            pltpu.VMEM((4, planes, spanwise), f32),
            pltpu.VMEM((2, group, LANES), f32),
            dma((planes // PIECE,)),
            dma((2,)),
            dma((2, components)),
            dma((2, components)),
            dma((2,)),
            dma((2,)),
            pltpu.VMEM((len(far_devices()), LANES), f32),
            pltpu.VMEM((1, LANES), f32),
            dma,
            dma,
            pltpu.SemaphoreType.REGULAR,
            pltpu.SemaphoreType.REGULAR,
        ],
        compiler_params=pltpu.CompilerParams(collective_id=0, has_side_effects=True, vmem_limit_bytes=24 * MIB),
        name="derive",
    )(*(
        pltpu.with_memory_space_constraint(operand, pltpu.HBM)
        for operand in (velocity.reshape(shape), jnp.asarray(matrix), jnp.asarray(columns))
    ))
    derivative, energy = pl.pallas_call(
        deliver,
        out_shape=(jax.ShapeDtypeStruct(shape, f32), jax.ShapeDtypeStruct((components, heights), f32)),
        in_specs=[near] * 2,
        out_specs=(far, far),
        scratch_shapes=[dma((2,))],
        compiler_params=pltpu.CompilerParams(vmem_limit_bytes=4 * MIB),
        name="deliver",
    )(derivative, energy)
    return derivative.reshape(velocity.shape), energy


def solution(mesh):
    return jax.shard_map(
        shards,
        mesh=mesh,
        in_specs=(P(None, None, "gx", "gz"),),
        out_specs=(P(None, None, "gx", "gz"), P()),
        check_vma=False,
    )
```

```python
import functools
import itertools
import math

import jax
import jax.numpy as jnp
import numpy as np
from jax import lax
from jax.experimental import pallas as pl
from jax.experimental.pallas import tpu as pltpu
from jax.sharding import PartitionSpec as P

ALPHA = 1.0 / 3.0
HALF_A = 7.0 / 9.0
QUARTER_B = 1.0 / 36.0

ROOT = (math.sqrt(1.0 - 4.0 * ALPHA * ALPHA) - 1.0) / (2.0 * ALPHA)
SCALE = 1.0 / math.sqrt(1.0 - 4.0 * ALPHA * ALPHA)
TAIL = SCALE * (HALF_A + QUARTER_B * (ROOT + 1.0 / ROOT))
CENTRE = SCALE * (HALF_A + 2.0 * QUARTER_B * ROOT)
BUMP = CENTRE - TAIL
REACH = 96

SIZES = {"x": 4, "y": 4, "z": 8, "core": 2}
PHASES = (("x", "y"), ("z", "core"))
AHEAD = (
    (0, 0, 0, 1), (0, 1, 0, 0), (0, 1, 0, 1), (0, 0, 1, 0), (0, 0, 1, 1), (1, 0, 0, 0), (1, 0, 0, 1),
    (0, 2, 0, 0), (0, 2, 0, 1), (0, 3, 0, 0), (0, 3, 0, 1), (0, 0, 2, 0), (0, 0, 2, 1),
    (0, 1, 1, 0), (0, 1, 1, 1), (1, 0, 1, 0), (1, 0, 1, 1),
)
FAR = range(3, 8)
MESH = pl.DeviceIdType.MESH
LANES = 128
ROW = SIZES["x"] * SIZES["core"]
PIECE = 4
GROUP = 12
MIB = 1024 * 1024


def around():
    gx, gz = lax.axis_index("gx"), lax.axis_index("gz")
    here = {"z": lax.div(gx, 4), "y": lax.rem(gx, 4), "x": lax.div(gz, 2), "core": lax.rem(gz, 2)}

    @functools.cache
    def moved(axis, offset):
        return lax.rem(here[axis] + offset, SIZES[axis]) if offset else here[axis]

    @functools.cache
    def paired(major, minor, one, two):
        if not (one or two):
            return gx if major == "z" else gz
        return moved(major, one) * SIZES[minor] + moved(minor, two)

    def at(x=0, y=0, z=0, core=0):
        return (
            paired("z", "y", z % SIZES["z"], y % SIZES["y"]),
            paired("x", "core", x % SIZES["x"], core % SIZES["core"]),
        )

    return at


def hops(offset, axis):
    return 0 if axis == "core" else min(offset, SIZES[axis] - offset)


def partners(at, axes):
    offsets = [o for o in itertools.product(*(range(SIZES[a]) for a in axes)) if any(o)]
    offsets.sort(key=lambda o: -sum(hops(v, a) for v, a in zip(o, axes)))
    return [at(**dict(zip(axes, offset))) for offset in offsets]


def place_of(x, y, z, core):
    return z * SIZES["y"] + y, x * SIZES["core"] + core


def far_devices(x=0, y=0):
    found = []
    for there in itertools.product(*(range(SIZES[a]) for a in ("x", "y")), FAR, range(SIZES["core"])):
        away = sum(hops(abs(to - at), a) for to, at, a in zip(there, (x, y), ("x", "y")))
        found.append((there[2], away, *place_of(*there)))
    return [tuple(there) for _, _, *there in sorted(found)]


def tables(points):
    index = np.arange(points)
    distance = np.abs(index[:, None] - index[None, :])
    matrix = np.where(distance == 0, CENTRE, TAIL * ROOT ** distance.astype(np.float64))
    matrix[:, 0] = 0.0
    matrix[:, points - 1] = 0.0
    reach = np.arange(REACH)
    powers = ROOT ** reach.astype(np.float64)
    head = ROOT**reach - ROOT ** (reach + 2.0)
    head[0], head[1] = 0.0, ROOT - ROOT**3
    columns = np.stack([powers, powers[::-1], head, -head[::-1]])
    columns = np.broadcast_to(columns[:, :, None], (4, REACH, LANES))
    return matrix.astype(np.float32), columns.astype(np.float32)


def column_sum(weights, block):
    w = jnp.concatenate([weights, weights], axis=1)
    return jnp.sum(w * block, axis=0, keepdims=True)


def derive(
    v_hbm, matrix_hbm, column_hbm, d_ref, e_ref,
    v, matrix, split, columns, out, got, rows, tots, shares, load_sem, const_sem, halo_send, halo_recv, sum_send, sum_recv,
    direct, total, direct_send, direct_recv, near_sem, mate_sem,
):
    planes, points, _ = v.shape
    parts, per_part = out.shape[1], out.shape[3]
    gx, gz = lax.axis_index("gx"), lax.axis_index("gz")
    ring = lax.axis_size("gx")
    sides = ((lax.rem(gx + ring - 1, ring), gz), (lax.rem(gx + 1, ring), gz))

    at = around()
    groups = [partners(at, axes) for axes in PHASES]

    shares[1] = jnp.zeros_like(shares[1])

    constants = [
        pltpu.make_async_copy(source, target, const_sem.at[i])
        for i, (source, target) in enumerate(((column_hbm, columns), (matrix_hbm, matrix)))
    ]

    def load(i):
        piece = pl.ds(i * PIECE, PIECE)
        return pltpu.make_async_copy(v_hbm.at[piece], v.at[piece], load_sem.at[i])

    constants[0].start()
    for i in range(planes // PIECE):
        load(i).start()
    constants[1].start()

    def signal(semaphore, there):
        pl.semaphore_signal(semaphore, inc=1, device_id=there, device_id_type=MESH)

    barrier = pltpu.get_barrier_semaphore()
    row, column = partners(at, ("x",)), partners(at, ("y",))
    levels = [at(z=offset) for offset in (2, -2, 1, -1)]
    mate = at(core=1)
    known = [*sides, *levels[:2], row[0], column[0], *levels[2:], *row[1:], *column[1:], mate]
    for there in known:
        signal(barrier, there)

    ahead = [place_of(*there) for there in AHEAD]
    is_ahead = functools.reduce(jnp.logical_or, ((gx == there[0]) & (gz == there[1]) for there in ahead))
    low, high_end = FAR.start * SIZES["y"], FAR.stop * SIZES["y"]
    is_far = (gx >= low) & (gx < high_end)

    for place, there in zip(AHEAD, ahead):

        @pl.when((gx == there[0]) & (gz == there[1]))
        def _(place=place):
            for target in far_devices(*place[:2]):
                signal(barrier, target)

    constants[0].wait()

    def summarise(part, k):
        p = part * per_part + k
        head, tail = v[p, :REACH, :], v[p, points - REACH :, :]
        first, second = head[0:1], head[1:2]
        last, before = tail[REACH - 1 :], tail[REACH - 2 : REACH - 1]
        one, row = pl.ds(p, 1), pl.ds(k, 1)
        out[0, part, 0, row, :] = first
        out[0, part, 1, row, :] = column_sum(columns[2], head - first)
        out[1, part, 0, row, :] = last
        out[1, part, 1, row, :] = column_sum(columns[3], tail - last)
        rows[0, one, :] = second
        rows[1, one, :] = before

    def halo(part, i):
        return pltpu.make_async_remote_copy(
            src_ref=out.at[i, part], dst_ref=got.at[1 - i, part],
            send_sem=halo_send.at[i, part], recv_sem=halo_recv.at[1 - i, part],
            device_id=sides[i], device_id_type=MESH,
        )

    for part in range(parts):

        def summarise_piece(i, carry):
            load(part * (per_part // PIECE) + i).wait()
            for k in range(PIECE):
                summarise(part, i * PIECE + k)
            return carry

        lax.fori_loop(0, per_part // PIECE, summarise_piece, 0)
        if part == parts - 2:
            pl.semaphore_wait(barrier, len(known) + len(AHEAD) * is_far.astype(jnp.int32))
        if part >= parts - 2:
            for ready in range(parts - 1) if part == parts - 2 else (part,):
                for i in range(2):
                    halo(ready, i).start()

    for there in row + levels[:2]:
        signal(near_sem, there)

    constants[1].wait()
    high = matrix[...].astype(jnp.bfloat16)
    split[:, :points] = (matrix[...] - high.astype(jnp.float32)).astype(jnp.bfloat16)
    split[:, points : 2 * points] = high
    split[:, 2 * points :] = high
    def solve(p):
        block = v[p]
        delta = pltpu.roll(block, points - 1, 0) - pltpu.roll(block, 1, 0)
        coarse = delta.astype(jnp.bfloat16)
        fine = (delta - coarse.astype(jnp.float32)).astype(jnp.bfloat16)
        local = jnp.dot(
            split[...], jnp.concatenate([coarse, fine, coarse], axis=0), preferred_element_type=jnp.float32
        )
        d_ref[p] = local
        one = pl.ds(p, 1)
        rows[2, one, :] = local[0:1]
        rows[3, one, :] = local[points - 1 :]
        rows[4, one, :] = column_sum(columns[0], local[:REACH])
        rows[5, one, :] = column_sum(columns[1], local[points - REACH :])
        rows[6, one, :] = jnp.sum(local * local, axis=0, keepdims=True)

    def solve_group(i, carry):
        for k in range(GROUP):
            solve(i * GROUP + k)
        return carry

    lax.fori_loop(0, planes // GROUP, solve_group, 0)

    squares = 1.0 / (1.0 - ROOT * ROOT)
    sums = []
    for part in range(parts):
        span = pl.ds(part * per_part, per_part)
        energy = rows[6, span, :]
        for i in range(2):
            halo(part, i).wait()
        for side, sign in ((0, 1.0), (1, -1.0)):
            own, inner, edge = out[side, part, 0], rows[side, span, :], got[side, part, 0]
            jump = sign * (inner - edge)
            reach_sum = jump + got[side, part, 1] + (sign * ROOT) * (own - edge)
            energy = energy + 2.0 * (TAIL * reach_sum * rows[4 + side, span, :] + BUMP * jump * rows[2 + side, span, :])
            energy = energy + (TAIL * TAIL * squares) * reach_sum * reach_sum
            energy = energy + (2.0 * TAIL * BUMP) * reach_sum * jump + (BUMP * BUMP) * jump * jump
            tots[side, span, :] = TAIL * reach_sum
            tots[2 + side, span, :] = BUMP * jump
        sums.append(jnp.sum(energy[:, :LANES] + energy[:, LANES:], axis=1, keepdims=True))

    chosen = lax.broadcasted_iota(jnp.int32, (planes, LANES), 0) == lax.broadcasted_iota(jnp.int32, (planes, LANES), 1)
    energy = jnp.broadcast_to(jnp.concatenate(sums, axis=0), (planes, LANES))
    share = jnp.sum(jnp.where(chosen, energy, 0.0), axis=0, keepdims=True)

    n_far = direct.shape[0]

    def send_direct(target):
        return pltpu.make_async_remote_copy(
            src_ref=shares.at[0, pl.ds(len(groups[0]), 1)], dst_ref=direct.at[pl.ds((gx - low) * ROW + gz, 1)],
            send_sem=direct_send, recv_sem=direct_recv, device_id=target, device_id_type=MESH,
        )

    def send_sum(phase, i):
        group = groups[phase]
        return pltpu.make_async_remote_copy(
            src_ref=shares.at[phase, pl.ds(len(group), 1)], dst_ref=shares.at[phase, pl.ds(i, 1)],
            send_sem=sum_send.at[phase], recv_sem=sum_recv.at[phase],
            device_id=group[i], device_id_type=MESH,
        )

    def rows_of(phase, count, semaphore):
        part = shares.at[phase, pl.ds(0, count)]
        return pltpu.make_async_copy(part, part, semaphore.at[phase])

    n_near, n_level = len(groups[0]), len(groups[1])
    skips = {}
    for x, y, _, _ in AHEAD:
        skips.setdefault((x, y), sum(place[:2] == (x, y) for place in AHEAD))
    here = lax.rem(gx, SIZES["y"]), lax.div(gz, SIZES["core"])
    skip = {xy: is_far & (here[0] == xy[1]) & (here[1] == xy[0]) for xy in skips}
    skips_none = jnp.logical_not(functools.reduce(jnp.logical_or, skip.values()))
    n_skip = len(FAR) * SIZES["core"]

    shares[0, n_near : n_near + 1, :] = share

    @pl.when(is_far)
    def _():
        send_direct(ahead[0]).start()

    pl.semaphore_wait(near_sem, len(row) + 2)
    for i in range(n_near):
        send_sum(0, i).start()

    @pl.when(is_far)
    def _():
        for target in ahead[1:]:
            send_direct(target).start()

    signal(mate_sem, mate)

    def correct(p, carry):
        one = pl.ds(p, 1)
        for side in range(2):
            wide = jnp.concatenate([columns[side], columns[side]], axis=1)
            place = pl.ds(0, REACH) if side == 0 else pl.ds(points - REACH, REACH)
            d_ref[p, place, :] = d_ref[p, place, :] + wide * tots[side, one, :]
        top, bottom = pl.ds(0, 1), pl.ds(points - 1, 1)
        d_ref[p, top, :] = d_ref[p, top, :] + tots[2, one, :]
        d_ref[p, bottom, :] = d_ref[p, bottom, :] + tots[3, one, :]
        return carry

    lax.fori_loop(0, planes, correct, 0)

    rows_of(0, n_near, sum_recv).wait()
    shares[1, n_level : n_level + 1, :] = jnp.sum(shares[0], axis=0, keepdims=True)
    pl.semaphore_wait(mate_sem, 1)
    @pl.when(skips_none)
    def _():
        for i in range(n_level):
            send_sum(1, i).start()

    for xy, condition in skip.items():

        @pl.when(condition)
        def _(xy=xy):
            kept = [there for place, there in zip(AHEAD, ahead) if place[:2] == xy]
            for i, there in enumerate(groups[1]):
                spared = functools.reduce(jnp.logical_or, ((there[0] == k[0]) & (there[1] == k[1]) for k in kept))

                @pl.when(jnp.logical_not(spared))
                def _(i=i):
                    send_sum(1, i).start()

    @pl.when(is_ahead)
    def _():
        rows_of(1, n_level - n_skip, sum_recv).wait()
        pltpu.make_async_copy(direct, direct, direct_recv).wait()
        total[...] = jnp.sum(jnp.concatenate([shares[1], direct[...]], axis=0), axis=0, keepdims=True)

    @pl.when(jnp.logical_not(is_ahead))
    def _():
        rows_of(1, n_level, sum_recv).wait()
        total[...] = jnp.sum(shares[1], axis=0, keepdims=True)

    count = float(points * ring * 2 * LANES * lax.axis_size("gz"))
    mean = total[...] * (1.0 / count)
    per_row = e_ref.shape[1]
    for i in range(e_ref.shape[0]):
        e_ref[i : i + 1, :] = mean[:, i * per_row : (i + 1) * per_row]
    rows_of(0, n_near, sum_send).wait()

    @pl.when(skips_none)
    def _():
        rows_of(1, n_level, sum_send).wait()

    for xy, condition in skip.items():

        @pl.when(condition)
        def _(xy=xy):
            rows_of(1, n_level - skips[xy], sum_send).wait()

    @pl.when(is_far)
    def _():
        part = direct.at[pl.ds(0, len(ahead))]
        pltpu.make_async_copy(part, part, direct_send).wait()


def deliver(d_vmem, e_vmem, d_hbm, e_hbm, sem):
    copies = [pltpu.make_async_copy(d_vmem, d_hbm, sem.at[0]), pltpu.make_async_copy(e_vmem, e_hbm, sem.at[1])]
    for copy in copies:
        copy.start()
    for copy in copies:
        copy.wait()


def shards(velocity):
    components, heights, points, spanwise = velocity.shape
    planes = components * heights
    shape = (planes, points, spanwise)
    matrix, columns = tables(points)
    f32, dma = jnp.float32, pltpu.SemaphoreType.DMA
    near, far = pl.BlockSpec(memory_space=pltpu.VMEM), pl.BlockSpec(memory_space=pltpu.HBM)
    halo = (2, components, 2, heights, spanwise)
    group = SIZES["x"] * SIZES["y"]

    derivative, energy = pl.pallas_call(
        derive,
        out_shape=(pltpu.VMEM(shape, f32), pltpu.VMEM((components, heights), f32)),
        in_specs=[far] * 3,
        out_specs=(near,) * 2,
        scratch_shapes=[
            pltpu.VMEM(shape, f32),
            pltpu.VMEM((points, points), f32),
            pltpu.VMEM((points, 3 * points), jnp.bfloat16),
            pltpu.VMEM(columns.shape, f32),
            pltpu.VMEM(halo, f32),
            pltpu.VMEM(halo, f32),
            pltpu.VMEM((7, planes, spanwise), f32),
            pltpu.VMEM((4, planes, spanwise), f32),
            pltpu.VMEM((2, group, LANES), f32),
            dma((planes // PIECE,)),
            dma((2,)),
            dma((2, components)),
            dma((2, components)),
            dma((2,)),
            dma((2,)),
            pltpu.VMEM((len(far_devices()), LANES), f32),
            pltpu.VMEM((1, LANES), f32),
            dma,
            dma,
            pltpu.SemaphoreType.REGULAR,
            pltpu.SemaphoreType.REGULAR,
        ],
        compiler_params=pltpu.CompilerParams(collective_id=0, has_side_effects=True, vmem_limit_bytes=24 * MIB),
        name="derive",
    )(*(
        pltpu.with_memory_space_constraint(operand, pltpu.HBM)
        for operand in (velocity.reshape(shape), jnp.asarray(matrix), jnp.asarray(columns))
    ))
    derivative, energy = pl.pallas_call(
        deliver,
        out_shape=(jax.ShapeDtypeStruct(shape, f32), jax.ShapeDtypeStruct((components, heights), f32)),
        in_specs=[near] * 2,
        out_specs=(far, far),
        scratch_shapes=[dma((2,))],
        compiler_params=pltpu.CompilerParams(vmem_limit_bytes=4 * MIB),
        name="deliver",
    )(derivative, energy)
    return derivative.reshape(velocity.shape), energy


def solution(mesh):
    return jax.shard_map(
        shards,
        mesh=mesh,
        in_specs=(P(None, None, "gx", "gz"),),
        out_specs=(P(None, None, "gx", "gz"), P()),
        check_vma=False,
    )
```
